32 devices in a mesh: outer: 8 (over z, x), inner: 4 (over y, core).
Axes of the slice: x: 2, y: 2, z: 4, core: 2. Of those that a mesh axis runs over, the one named last changes fastest.
Arguments:
- activations: bfloat16 [8192, 8192], P(('outer', 'inner')), may hold values from -6 to 6
- output_grads: bfloat16 [8192, 512], P(('outer', 'inner')), may hold values from -0.06591797 to 0.06591797
- master_weights: float32 [8192, 512], P(('inner', 'outer')), may hold values from -0.0625 to 0.0625
- first_moment: float32 [8192, 512], P(('inner', 'outer')), may hold values from -5 to 5
- second_moment: float32 [8192, 512], P(('inner', 'outer')), may hold values from 0.1 to 2
- next_tokens: bfloat16 [8192, 8192], P(('outer', 'inner')), may hold values from -6 to 6
Outputs:
- new_master: float32 [8192, 512], P(('inner', 'outer'))
- new_first_moment: float32 [8192, 512], P(('inner', 'outer'))
- new_second_moment: float32 [8192, 512], P(('inner', 'outer'))
- kept_weights: bfloat16 [8192, 512], P('inner')
- projection: bfloat16 [8192, 512], P(('outer', 'inner'))
The draws below stay inside these ranges and needn't reach their ends.
All inputs are finite; a program needn't handle non-finite values.
Results may differ from the reference program's by a relative error of at most 0.012.
Values may be sent and summed in bfloat16 or wider, within the bound.
A program may use at most 128 MiB of HBM per device.

```python
import math
import jax
import jax.numpy as jnp
from jax import lax

D = 8192
TOK_DEV = 256
ADAM_STEP = 10
KEY_COLS = 512
TOKENS = 8192


def raised(entries, stream_key, source, target, blocks, factor):
    def block_of(position):
        return (jnp.arange(entries.shape[position]) // (entries.shape[position] // blocks)).reshape((-1,) + (1,) * (entries.ndim - 1 - position))

    near = jax.random.permutation(stream_key, blocks)[block_of(target)]
    second = (block_of(target) + blocks // 2) % blocks
    return jnp.where((block_of(source) == near) | (block_of(source) == second), factor * entries, entries)


def levels(stream_key, extent, pieces, smallest, largest):
    level, own = 1.0, jax.random.fold_in(stream_key, 6)
    for axis_at, blocks in pieces:
        heights = jnp.exp(jax.random.uniform(jax.random.fold_in(own, axis_at), (blocks,), jnp.float32, smallest / len(pieces), largest / len(pieces)))
        level = level * jnp.repeat(heights, extent[axis_at] // blocks).reshape([-1 if axis == axis_at else 1 for axis in range(len(extent))])
    return level


def bell_draw(stream_key, extent, spread, most, split=(), dtype=jnp.bfloat16):
    array = jax.random.normal(stream_key, extent, jnp.float32) * spread
    if len(split) > 0:
        array = levels(stream_key, extent, split, -0.22, 0.18) * array
    return jnp.clip(array, min=-most, max=most).astype(dtype)


def heavy_noise(key, extent, deviation, reach, split, heavy, kind=jnp.bfloat16):
    drawn = deviation * jax.random.normal(key, extent, jnp.float32)
    if split:
        drawn = drawn * levels(key, extent, split, -0.22, 0.18)
    return jnp.clip(raised(drawn, jax.random.fold_in(key, 3), *heavy), -reach, reach).astype(kind)


def setup_inputs(seed: int = 0) -> dict:
    key_of = jax.random.split(jax.random.key(seed), 7)
    return {
        "activations": heavy_noise(key_of[0], (TOKENS, D), 1.0, 6.0, ((0, 32),), (0, 1, 32, 2.75)),
        "output_grads": bell_draw(key_of[1], (TOKENS, KEY_COLS), (TOKENS ** -0.5), 0.06591797, ((0, 32),)),
        "master_weights": bell_draw(key_of[2], (D, KEY_COLS), D ** -0.5, 0.0625, ((0, 32),), jnp.float32),
        "first_moment": bell_draw(key_of[3], (D, KEY_COLS), 1.0, 5.0, ((0, 32),), jnp.float32),
        "second_moment": jnp.clip(jnp.exp(math.log(2.0) - 2.9957323 * jax.random.uniform(key_of[4], (D, KEY_COLS), jnp.float32) ** levels(key_of[4], (D, KEY_COLS), ((0, 32),), -0.2, 0.2)), 0.1, 2.0),
        "next_tokens": bell_draw(key_of[5], (TOKENS, D), 1.0, 6.0, ((0, 32),)),
    }


beta_first = 0.9
beta_second = 0.95
learn_rate = 0.002
decay_rate = 0.1
adam_eps = 1e-08

def adamw_update(gradient, master_weights, first_moment, second_moment):
    new_first = beta_first * first_moment + (1.0 - beta_first) * gradient
    new_second = beta_second * second_moment + (1.0 - beta_second) * gradient * gradient
    first_hat = new_first / (1.0 - beta_first ** ADAM_STEP)
    second_hat = new_second / (1.0 - beta_second ** ADAM_STEP)
    new_master = master_weights - learn_rate * (first_hat / (jnp.sqrt(second_hat) + adam_eps) + decay_rate * master_weights)
    return (new_master, new_first, new_second)

def reference(activations, output_grads, master_weights, first_moment, second_moment, next_tokens):
    block_count = TOKENS // TOK_DEV
    act_blocks = activations.reshape(block_count, TOK_DEV, D)
    grad_blocks = output_grads.reshape(block_count, TOK_DEV, KEY_COLS)

    def accumulate(running, inputs):
        block_act, block_grad = inputs
        contrib = jnp.einsum('tr,tc->rc', block_act, block_grad, preferred_element_type=jnp.float32).astype(jnp.bfloat16)
        contrib = lax.optimization_barrier(contrib)
        return (running + contrib.astype(jnp.float32), None)
    gradient, _ = lax.scan(accumulate, jnp.zeros((D, KEY_COLS), jnp.float32), (act_blocks, grad_blocks))
    new_master, new_first, new_second = adamw_update(gradient, master_weights, first_moment, second_moment)
    kept_weights = new_master.astype(jnp.bfloat16)
    projection = jnp.dot(next_tokens, kept_weights, preferred_element_type=jnp.float32).astype(jnp.bfloat16)
    return (new_master, new_first, new_second, kept_weights, projection)
```

```python
import functools

import jax
import jax.numpy as jnp
from jax import lax
from jax.experimental import pallas as pl
from jax.experimental.pallas import tpu as pltpu
from jax.sharding import PartitionSpec as P

ADAM_STEP = 10
MESH = pl.DeviceIdType.MESH
BF16 = jnp.bfloat16
F32 = jnp.float32


beta_first = 0.9
beta_second = 0.95
learn_rate = 0.002
decay_rate = 0.1
adam_eps = 1e-08


def adamw_update(gradient, master_weights, first_moment, second_moment):
    new_first = beta_first * first_moment + (1.0 - beta_first) * gradient
    new_second = beta_second * second_moment + (1.0 - beta_second) * gradient * gradient
    first_hat = new_first / (1.0 - beta_first**ADAM_STEP)
    second_hat = new_second / (1.0 - beta_second**ADAM_STEP)
    new_master = master_weights - learn_rate * (
        first_hat / (jnp.sqrt(second_hat) + adam_eps) + decay_rate * master_weights
    )
    return (new_master, new_first, new_second)


def rounded_term(columns, output_grads):
    contrib = jnp.einsum(
        "tr,tc->rc", columns, output_grads, preferred_element_type=jnp.float32
    ).astype(jnp.bfloat16)
    contrib = lax.optimization_barrier(contrib)
    return contrib.astype(jnp.float32)


def regroup_features(activations, outer_count, inner_count):
    tok_rows, width = activations.shape
    shard_rows = width // (outer_count * inner_count)
    split_view = activations.reshape(tok_rows, inner_count, outer_count, shard_rows)
    return split_view.transpose(0, 2, 1, 3).reshape(tok_rows, width)


def local_plain(activations, output_grads, master_weights, first_moment, second_moment, next_tokens):
    outer_count = lax.axis_size("outer")
    inner_count = lax.axis_size("inner")
    regrouped = regroup_features(activations, outer_count, inner_count)
    gradient = lax.psum_scatter(
        rounded_term(regrouped, output_grads), ("outer", "inner"), scatter_dimension=0, tiled=True
    )
    new_master, new_first, new_second = adamw_update(
        gradient, master_weights, first_moment, second_moment
    )
    kept_shard = new_master.astype(jnp.bfloat16)
    kept_weights = lax.all_gather(kept_shard, "outer", axis=0, tiled=True)
    projected = jnp.dot(
        next_tokens,
        lax.all_gather(kept_weights, "inner", axis=0, tiled=True),
        preferred_element_type=jnp.float32,
    )
    return (new_master, new_first, new_second, kept_weights, projected.astype(jnp.bfloat16))


class Plan:
    def __init__(self, n_out, n_in, rows, cols):
        self.n_out, self.n_in, self.rows, self.cols = n_out, n_in, rows, cols
        out_bits = [("outer", k) for k in range(n_out.bit_length() - 1)]
        in_bits = [("inner", k) for k in range(1, n_in.bit_length() - 1)]
        ranked = []
        for k in range(max(len(out_bits), len(in_bits))):
            ranked += out_bits[k : k + 1] + in_bits[k : k + 1]
        self.dims = ranked[::-1]
        self.depth = len(ranked)
        self.blocks = 2**self.depth
        top = self.depth - 1
        first = tuple(range(top, -1, -1))
        second = (top - 1, top) + first[2:]
        self.parts = [
            (first, (0, cols // 2), (0, rows // 2)),
            (second, (cols // 2, cols // 2), (rows // 2, rows // 2)),
        ]

    def canon(self, p, k):
        order = self.parts[p][0]
        return sum(((k >> t) & 1) << order[self.depth - 1 - t] for t in range(self.depth))


def kernel(plan, *refs):
    (act_h, grad_h, mw_h, m1_h, m2_h, nt_h, nm_o, n1_o, n2_o, kept_o, proj_o) = refs[:11]
    (act, grad, nt, mw, m1, m2, nm, n1, n2, grad_t, own, snd0, rcv0, total, weights, acc) = refs[11:27]
    n_parts, depth, blocks = len(plan.parts), plan.depth, plan.blocks
    rv_flat = refs[27 : 27 + n_parts * depth]
    (core_send, core_recv, rs_send, rs_recv, ag_send, ag_recv, cg_send, cg_recv, local) = refs[
        27 + n_parts * depth :
    ]
    rv = [rv_flat[p * depth : (p + 1) * depth] for p in range(n_parts)]
    R, C = plan.rows, plan.cols

    loads = [
        pltpu.make_async_copy(s, d, local.at[i])
        for i, (s, d) in enumerate(
            [(grad_h, grad), (act_h, act), (mw_h, mw), (m1_h, m1), (m2_h, m2), (nt_h, nt)]
        )
    ]
    for load in loads:
        load.start()

    outer, inner = lax.axis_index("outer"), lax.axis_index("inner")
    place = {"outer": outer, "inner": inner}

    def bit(axis, k):
        return (place[axis] // 2**k) % 2

    def partner(axis, k):
        other = place[axis] + (1 - 2 * bit(axis, k)) * 2**k
        return (other, inner) if axis == "outer" else (outer, other)

    sibling = partner("inner", 0)
    others = [partner(axis, k) for axis, k in plan.dims]

    barrier = pltpu.get_barrier_semaphore()
    for device in [sibling] + others:
        pl.semaphore_signal(barrier, inc=1, device_id=device, device_id_type=MESH)

    def block_at(flip_core, c):
        o, n = outer, inner
        if flip_core:
            n = n + 1 - 2 * bit("inner", 0)
        for j, (axis, k) in enumerate(plan.dims):
            step = ((c // 2**j) % 2) * (1 - 2 * bit(axis, k)) * 2**k
            if axis == "outer":
                o = o + step
            else:
                n = n + step
        return o, n

    def columns(flip_core, c):
        o, n = block_at(flip_core, c)
        return pl.ds(pl.multiple_of((n * plan.n_out + o) * R, R), R)

    loads[0].wait()
    grad_t[...] = grad[...].astype(F32).T.astype(BF16)
    loads[1].wait()
    pl.semaphore_wait(barrier, 1 + depth)

    def core_copy(c):
        return pltpu.make_async_remote_copy(
            src_ref=snd0.at[c],
            dst_ref=rcv0.at[c],
            send_sem=core_send.at[c],
            recv_sem=core_recv.at[c],
            device_id=sibling,
            device_id_type=MESH,
        )

    @pl.loop(0, blocks)
    def _(i):
        c = blocks - 1 - i
        snd0[c] = jnp.dot(
            grad_t[...], act[:, columns(True, c)], preferred_element_type=F32
        ).astype(BF16)
        core_copy(c).start()

    @pl.loop(0, blocks)
    def _(i):
        c = blocks - 1 - i
        own[c] = jnp.dot(
            grad_t[...], act[:, columns(False, c)], preferred_element_type=F32
        ).astype(BF16)

    sums = {}
    arrived = set()

    def need(key, copy):
        if key not in arrived:
            arrived.add(key)
            copy.wait_recv()

    tile = 64

    def gather_terms(p, k, steps, dst, dst_dtype):
        _, (lo, count), _ = plan.parts[p]
        c = plan.canon(p, k)
        need(("core", c), core_copy(c))
        for t in range(steps):
            need((p, t, k), sums[(p, k + 2 ** (depth - 1 - t))])

        @pl.loop(0, count // tile)
        def _(i):
            at = pl.multiple_of(i * tile, tile)
            span = pl.ds(lo + at, tile)
            value = own[c, span, :].astype(F32) + rcv0[c, span, :].astype(F32)
            for t in range(steps):
                value += rv[p][t][k, pl.ds(at, tile), :].astype(F32)
            if dst is None:
                own[c, span, :] = value.astype(dst_dtype)
            else:
                dst[span, :] = value

    for k in range(blocks - 1, 0, -1):
        for p in range(n_parts):
            order, (lo, count), _ = plan.parts[p]
            high = k.bit_length() - 1
            step = depth - 1 - high
            gather_terms(p, k, step, None, BF16)
            c = plan.canon(p, k)
            copy = pltpu.make_async_remote_copy(
                src_ref=own.at[c, pl.ds(lo, count)],
                dst_ref=rv[p][step].at[k - 2**high],
                send_sem=rs_send.at[p, k],
                recv_sem=rs_recv.at[p, k],
                device_id=others[order[step]],
                device_id_type=MESH,
            )
            copy.start()
            sums[(p, k)] = copy
    for p in range(n_parts):
        gather_terms(p, 0, depth, total, F32)

    for load in loads[2:5]:
        load.wait()
    half = R // n_parts
    for p in range(n_parts):
        lo = p * half
        gradient = total[:, lo : lo + half].T
        span = pl.ds(lo, half)
        master, first, second = adamw_update(gradient, mw[span, :], m1[span, :], m2[span, :])
        nm[span, :] = master
        n1[span, :] = first
        n2[span, :] = second
        weights[0, 0, span, :] = master.astype(BF16)

    stores = [
        pltpu.make_async_copy(s, d, local.at[6 + i])
        for i, (s, d) in enumerate([(nm, nm_o), (n1, n1_o), (n2, n2_o)])
    ]
    for store in stores:
        store.start()

    acc[...] = jnp.zeros_like(acc)
    loads[5].wait()

    def project(side, c):
        acc[...] += jnp.dot(
            nt[:, columns(side == 1, c)], weights[side, c], preferred_element_type=F32
        )

    passed, crossed, keeps = {}, {}, []
    have = {c: 0 for c in range(blocks)}
    inner_mask = sum(2**j for j, (axis, _) in enumerate(plan.dims) if axis == "inner")
    pending = []

    def finish_sibling(c):
        for p in range(n_parts):
            crossed[(p, c)].wait_recv()
        project(1, c)

    for q in range(blocks):
        ready = []
        for p in range(n_parts):
            order, _, (lo, count) = plan.parts[p]
            c = plan.canon(p, q)
            high = q.bit_length() - 1
            if q > 0:
                passed[(p, q - 2**high, high)].wait_recv()
            rows = pl.ds(lo, count)
            for t in range(high + 1, depth):
                e = order[depth - 1 - t]
                copy = pltpu.make_async_remote_copy(
                    src_ref=weights.at[0, c, rows],
                    dst_ref=weights.at[0, c + 2**e, rows],
                    send_sem=ag_send.at[p, q + 2**t],
                    recv_sem=ag_recv.at[p, q + 2**t],
                    device_id=others[e],
                    device_id_type=MESH,
                )
                copy.start()
                passed[(p, q, t)] = copy
            copy = pltpu.make_async_remote_copy(
                src_ref=weights.at[0, c, rows],
                dst_ref=weights.at[1, c, rows],
                send_sem=cg_send.at[p, c],
                recv_sem=cg_recv.at[p, c],
                device_id=sibling,
                device_id_type=MESH,
            )
            copy.start()
            crossed[(p, c)] = copy
            have[c] += 1
            if have[c] == n_parts:
                ready.append(c)
        for c in ready:
            if c & inner_mask == 0:
                o, _ = block_at(False, c)
                keep = pltpu.make_async_copy(
                    weights.at[0, c],
                    kept_o.at[pl.ds(pl.multiple_of(o * R, R), R)],
                    local.at[9 + len(keeps)],
                )
                keep.start()
                keeps.append(keep)
            project(0, c)
            pending.append(c)
        while len(pending) > 2:
            finish_sibling(pending.pop(0))
    for c in pending:
        finish_sibling(c)
    proj_o[...] = acc[...].astype(BF16)

    for c in range(blocks):
        core_copy(c).wait_send()
    for copy in list(sums.values()) + list(passed.values()) + list(crossed.values()):
        copy.wait_send()
    for copy in stores + keeps:
        copy.wait()


def local_kernel(activations, output_grads, master_weights, first_moment, second_moment, next_tokens):
    n_out, n_in = lax.axis_size("outer"), lax.axis_size("inner")
    tokens, width = activations.shape
    next_rows = next_tokens.shape[0]
    R, C = master_weights.shape
    plan = Plan(n_out, n_in, R, C)
    B, L, n_parts = plan.blocks, plan.depth, len(plan.parts)
    dma = pltpu.SemaphoreType.DMA
    any_spec = pl.BlockSpec(memory_space=pl.ANY)
    arrived = [
        pltpu.VMEM((2 ** (L - 1 - s), count, R), BF16)
        for _, (_, count), _ in plan.parts
        for s in range(L)
    ]
    return pl.pallas_call(
        functools.partial(kernel, plan),
        out_shape=(
            jax.ShapeDtypeStruct((R, C), F32),
            jax.ShapeDtypeStruct((R, C), F32),
            jax.ShapeDtypeStruct((R, C), F32),
            jax.ShapeDtypeStruct((n_out * R, C), BF16),
            jax.ShapeDtypeStruct((next_rows, C), BF16),
        ),
        in_specs=[any_spec] * 6,
        out_specs=(any_spec,) * 4 + (pl.BlockSpec(memory_space=pltpu.VMEM),),
        scratch_shapes=[
            pltpu.VMEM((tokens, width), BF16),
            pltpu.VMEM((tokens, C), BF16),
            pltpu.VMEM((next_rows, width), BF16),
        ]
        + [pltpu.VMEM((R, C), F32)] * 6
        + [
            pltpu.VMEM((C, tokens), BF16),
            pltpu.VMEM((B, C, R), BF16),
            pltpu.VMEM((B, C, R), BF16),
            pltpu.VMEM((B, C, R), BF16),
            pltpu.VMEM((C, R), F32),
            pltpu.VMEM((2, B, R, C), BF16),
            pltpu.VMEM((next_rows, C), F32),
        ]
        + arrived
        + [
            dma((B,)),
            dma((B,)),
            dma((n_parts, B)),
            dma((n_parts, B)),
            dma((n_parts, B)),
            dma((n_parts, B)),
            dma((n_parts, B)),
            dma((n_parts, B)),
            dma((9 + n_out,)),
        ],
        compiler_params=pltpu.CompilerParams(
            collective_id=0, has_side_effects=True, vmem_limit_bytes=58 * 2**20
        ),
        cost_estimate=pl.CostEstimate(
            flops=2 * (tokens + next_rows) * width * C,
            bytes_accessed=2 * (tokens + next_rows) * width + 24 * R * C,
            transcendentals=R * C,
        ),
    )(activations, output_grads, master_weights, first_moment, second_moment, next_tokens)


def fits_kernel(mesh):
    n_out, n_in = mesh.shape["outer"], mesh.shape["inner"]
    powers = n_out & (n_out - 1) == 0 and n_in & (n_in - 1) == 0
    return powers and n_out >= 2 and n_in >= 4 and n_out * n_in <= 32


def solution(mesh):
    placed = (
        P(("outer", "inner"), None),
        P(("outer", "inner"), None),
        P(("inner", "outer"), None),
        P(("inner", "outer"), None),
        P(("inner", "outer"), None),
        P(("outer", "inner"), None),
    )
    return jax.shard_map(
        local_kernel if fits_kernel(mesh) else local_plain,
        mesh=mesh,
        in_specs=placed,
        out_specs=(
            P(("inner", "outer"), None),
            P(("inner", "outer"), None),
            P(("inner", "outer"), None),
            P("inner", None),
            P(("outer", "inner"), None),
        ),
        check_vma=False,
    )
```

```python
import functools

import jax
import jax.numpy as jnp
from jax import lax
from jax.experimental import pallas as pl
from jax.experimental.pallas import tpu as pltpu
from jax.sharding import PartitionSpec as P

ADAM_STEP = 10
MESH = pl.DeviceIdType.MESH
BF16 = jnp.bfloat16
F32 = jnp.float32


beta_first = 0.9
beta_second = 0.95
learn_rate = 0.002
decay_rate = 0.1
adam_eps = 1e-08


def adamw_update(gradient, master_weights, first_moment, second_moment):
    new_first = beta_first * first_moment + (1.0 - beta_first) * gradient
    new_second = beta_second * second_moment + (1.0 - beta_second) * gradient * gradient
    first_hat = new_first / (1.0 - beta_first**ADAM_STEP)
    second_hat = new_second / (1.0 - beta_second**ADAM_STEP)
    new_master = master_weights - learn_rate * (
        first_hat / (jnp.sqrt(second_hat) + adam_eps) + decay_rate * master_weights
    )
    return (new_master, new_first, new_second)


def rounded_term(columns, output_grads):
    contrib = jnp.einsum(
        "tr,tc->rc", columns, output_grads, preferred_element_type=jnp.float32
    ).astype(jnp.bfloat16)
    contrib = lax.optimization_barrier(contrib)
    return contrib.astype(jnp.float32)


def regroup_features(activations, outer_count, inner_count):
    tok_rows, width = activations.shape
    shard_rows = width // (outer_count * inner_count)
    split_view = activations.reshape(tok_rows, inner_count, outer_count, shard_rows)
    return split_view.transpose(0, 2, 1, 3).reshape(tok_rows, width)


def local_plain(activations, output_grads, master_weights, first_moment, second_moment, next_tokens):
    outer_count = lax.axis_size("outer")
    inner_count = lax.axis_size("inner")
    regrouped = regroup_features(activations, outer_count, inner_count)
    gradient = lax.psum_scatter(
        rounded_term(regrouped, output_grads), ("outer", "inner"), scatter_dimension=0, tiled=True
    )
    new_master, new_first, new_second = adamw_update(
        gradient, master_weights, first_moment, second_moment
    )
    kept_shard = new_master.astype(jnp.bfloat16)
    kept_weights = lax.all_gather(kept_shard, "outer", axis=0, tiled=True)
    projected = jnp.dot(
        next_tokens,
        lax.all_gather(kept_weights, "inner", axis=0, tiled=True),
        preferred_element_type=jnp.float32,
    )
    return (new_master, new_first, new_second, kept_weights, projected.astype(jnp.bfloat16))


SUM_ORDERS = [((3, 0, 2, 1), 1), ((2, 1, 3, 0), 1)]
GATHER_ORDERS = [((3, 1, 2, 0), 1), ((2, 0, 3, 1), 1)]


class Plan:
    def __init__(self, n_out, n_in, rows, cols):
        self.n_out, self.n_in, self.rows, self.cols = n_out, n_in, rows, cols
        out_bits = [("outer", k) for k in range(n_out.bit_length() - 1)]
        in_bits = [("inner", k) for k in range(1, n_in.bit_length() - 1)]
        ranked = []
        for k in range(max(len(out_bits), len(in_bits))):
            ranked += out_bits[k : k + 1] + in_bits[k : k + 1]
        self.dims = ranked[::-1]
        self.depth = len(ranked)
        self.blocks = 2**self.depth
        self.sum_parts = self.cut(cols, SUM_ORDERS)
        self.keep_parts = self.cut(rows, GATHER_ORDERS)

    def cut(self, extent, orders):
        plain = tuple(range(self.depth - 1, -1, -1))
        share = sum(weight for _, weight in orders)
        parts, lo = [], 0
        for order, weight in orders:
            count = extent * weight // share
            parts.append((order if self.depth == len(order) else plain, lo, count))
            lo += count
        return parts

    def canon(self, order, k):
        return sum(((k >> t) & 1) << order[self.depth - 1 - t] for t in range(self.depth))


def kernel(plan, *refs):
    (act_h, grad_h, mw_h, m1_h, m2_h, nt_h, nm_o, n1_o, n2_o, kept_o, proj_o) = refs[:11]
    (act, grad, nt, mw, m1, m2, nm, n1, n2, grad_t, own, snd0, rcv0, total, weights, acc) = refs[11:27]
    depth, blocks = plan.depth, plan.blocks
    sum_parts, keep_parts = plan.sum_parts, plan.keep_parts
    rv_flat = refs[27 : 27 + len(sum_parts) * depth]
    (
        load_sem,
        core_send,
        core_recv,
        rs_send,
        rs_recv,
        ag_send,
        ag_recv,
        cg_send,
        cg_recv,
        local,
    ) = refs[27 + len(sum_parts) * depth :]
    rv = [rv_flat[p * depth : (p + 1) * depth] for p in range(len(sum_parts))]
    R, C = plan.rows, plan.cols

    outer, inner = lax.axis_index("outer"), lax.axis_index("inner")
    place = {"outer": outer, "inner": inner}

    def bit(axis, k):
        return (place[axis] // 2**k) % 2

    def partner(axis, k):
        other = place[axis] + (1 - 2 * bit(axis, k)) * 2**k
        return (other, inner) if axis == "outer" else (outer, other)

    sibling = partner("inner", 0)
    others = [partner(axis, k) for axis, k in plan.dims]

    barrier = pltpu.get_barrier_semaphore()
    for device in [sibling] + others:
        pl.semaphore_signal(barrier, inc=1, device_id=device, device_id_type=MESH)

    def block_at(flip_core, c):
        o, n = outer, inner
        if flip_core:
            n = n + 1 - 2 * bit("inner", 0)
        for j, (axis, k) in enumerate(plan.dims):
            step = ((c // 2**j) % 2) * (1 - 2 * bit(axis, k)) * 2**k
            if axis == "outer":
                o = o + step
            else:
                n = n + step
        return o, n

    def columns(flip_core, c):
        o, n = block_at(flip_core, c)
        return pl.ds(pl.multiple_of((n * plan.n_out + o) * R, R), R)

    sequence = []
    for k in range(blocks - 1, -1, -1):
        for order, _, _ in sum_parts:
            c = plan.canon(order, k)
            if k >= blocks // 2 and c not in sequence:
                sequence.append(c)
    sequence += [c for c in range(blocks - 1, -1, -1) if c not in sequence]

    first_load = pltpu.make_async_copy(grad_h, grad, local.at[0])
    first_load.start()
    act_loads = {}
    for c in sequence:
        for side in (1, 0):
            load = pltpu.make_async_copy(
                act_h.at[:, columns(side == 1, c)], act.at[side, c], load_sem.at[side, c]
            )
            load.start()
            act_loads[(side, c)] = load
    loads = [
        pltpu.make_async_copy(s, d, local.at[1 + i])
        for i, (s, d) in enumerate([(mw_h, mw), (m1_h, m1), (m2_h, m2), (nt_h, nt)])
    ]
    for load in loads:
        load.start()

    first_load.wait()
    grad_t[...] = grad[...].astype(F32).T.astype(BF16)

    cores = {}

    def term(side, c):
        act_loads[(side, c)].wait()
        return jnp.dot(grad_t[...], act[side, c], preferred_element_type=F32).astype(BF16)

    def send_term(c):
        snd0[c] = term(1, c)
        copy = pltpu.make_async_remote_copy(
            src_ref=snd0.at[c],
            dst_ref=rcv0.at[c],
            send_sem=core_send.at[c],
            recv_sem=core_recv.at[c],
            device_id=sibling,
            device_id_type=MESH,
        )
        copy.start()
        cores[c] = copy

    sums = {}
    arrived = set()
    tile = 64

    def gather_terms(p, k, steps, dst):
        order, lo, count = sum_parts[p]
        c = plan.canon(order, k)
        if c not in arrived:
            arrived.add(c)
            cores[c].wait_recv()
        for t in range(steps):
            sums[(p, k + 2 ** (depth - 1 - t))].wait_recv()

        @pl.loop(0, count // tile)
        def _(i):
            at = pl.multiple_of(i * tile, tile)
            span = pl.ds(lo + at, tile)
            value = own[c, span, :].astype(F32) + rcv0[c, span, :].astype(F32)
            for t in range(steps):
                value += rv[p][t][k, pl.ds(at, tile), :].astype(F32)
            if dst is None:
                own[c, span, :] = value.astype(BF16)
            else:
                dst[span, :] = value

    def send_sum(p, k):
        order, lo, count = sum_parts[p]
        high = k.bit_length() - 1
        step = depth - 1 - high
        gather_terms(p, k, step, None)
        copy = pltpu.make_async_remote_copy(
            src_ref=own.at[plan.canon(order, k), pl.ds(lo, count)],
            dst_ref=rv[p][step].at[k - 2**high],
            send_sem=rs_send.at[p, k],
            recv_sem=rs_recv.at[p, k],
            device_id=others[order[step]],
            device_id_type=MESH,
        )
        copy.start()
        sums[(p, k)] = copy

    pl.semaphore_wait(barrier, 1 + depth)
    lag = 2
    for n in range(blocks + lag):
        if n < blocks:
            c = sequence[n]
            send_term(c)
            own[c] = term(0, c)
        if n >= lag:
            for p, (order, _, _) in enumerate(sum_parts):
                for k in range(blocks - 1, blocks // 2 - 1, -1):
                    if plan.canon(order, k) == sequence[n - lag]:
                        send_sum(p, k)
    for k in range(blocks // 2 - 1, 0, -1):
        for p in range(len(sum_parts)):
            send_sum(p, k)
    for p in range(len(sum_parts)):
        gather_terms(p, 0, depth, total)

    def update(lo, count):
        gradient = total[:, lo : lo + count].T
        span = pl.ds(lo, count)
        master, first, second = adamw_update(gradient, mw[span, :], m1[span, :], m2[span, :])
        nm[span, :] = master
        n1[span, :] = first
        n2[span, :] = second
        weights[0, 0, span, :] = master.astype(BF16)

    for load in loads[:3]:
        load.wait()

    def project(side, c):
        acc[...] += jnp.dot(
            nt[:, columns(side == 1, c)], weights[side, c], preferred_element_type=F32
        )

    passed, crossed, keeps = {}, {}, []
    have = {c: 0 for c in range(blocks)}
    inner_mask = sum(2**j for j, (axis, _) in enumerate(plan.dims) if axis == "inner")
    pending = []

    def finish_sibling(c):
        for p in range(len(keep_parts)):
            crossed[(p, c)].wait_recv()
        project(1, c)

    for q in range(blocks):
        ready = []
        for p, (order, lo, count) in enumerate(keep_parts):
            c = plan.canon(order, q)
            if q == 0:
                update(lo, count)
            high = q.bit_length() - 1
            if q > 0:
                passed[(p, q - 2**high, high)].wait_recv()
            rows = pl.ds(lo, count)
            for t in range(high + 1, depth):
                e = order[depth - 1 - t]
                copy = pltpu.make_async_remote_copy(
                    src_ref=weights.at[0, c, rows],
                    dst_ref=weights.at[0, c + 2**e, rows],
                    send_sem=ag_send.at[p, q + 2**t],
                    recv_sem=ag_recv.at[p, q + 2**t],
                    device_id=others[e],
                    device_id_type=MESH,
                )
                copy.start()
                passed[(p, q, t)] = copy
            copy = pltpu.make_async_remote_copy(
                src_ref=weights.at[0, c, rows],
                dst_ref=weights.at[1, c, rows],
                send_sem=cg_send.at[p, c],
                recv_sem=cg_recv.at[p, c],
                device_id=sibling,
                device_id_type=MESH,
            )
            copy.start()
            crossed[(p, c)] = copy
            have[c] += 1
            if have[c] == len(keep_parts):
                ready.append(c)
        if q == 0:
            stores = [
                pltpu.make_async_copy(s, d, local.at[5 + i])
                for i, (s, d) in enumerate([(nm, nm_o), (n1, n1_o), (n2, n2_o)])
            ]
            for store in stores:
                store.start()
            acc[...] = jnp.zeros_like(acc)
            loads[3].wait()
        for c in ready:
            if c & inner_mask == 0:
                o, _ = block_at(False, c)
                keep = pltpu.make_async_copy(
                    weights.at[0, c],
                    kept_o.at[pl.ds(pl.multiple_of(o * R, R), R)],
                    local.at[8 + len(keeps)],
                )
                keep.start()
                keeps.append(keep)
            project(0, c)
            pending.append(c)
        while len(pending) > 2:
            finish_sibling(pending.pop(0))
    for c in pending:
        finish_sibling(c)
    proj_o[...] = acc[...].astype(BF16)

    for copy in list(cores.values()) + list(sums.values()) + list(passed.values()) + list(crossed.values()):
        copy.wait_send()
    for copy in stores + keeps:
        copy.wait()


def local_kernel(activations, output_grads, master_weights, first_moment, second_moment, next_tokens):
    n_out, n_in = lax.axis_size("outer"), lax.axis_size("inner")
    tokens, width = activations.shape
    next_rows = next_tokens.shape[0]
    R, C = master_weights.shape
    plan = Plan(n_out, n_in, R, C)
    B, L = plan.blocks, plan.depth
    n_sum, n_keep = len(plan.sum_parts), len(plan.keep_parts)
    dma = pltpu.SemaphoreType.DMA
    any_spec = pl.BlockSpec(memory_space=pl.ANY)
    arrived = [
        pltpu.VMEM((2 ** (L - 1 - s), count, R), BF16)
        for _, _, count in plan.sum_parts
        for s in range(L)
    ]
    results = pl.pallas_call(
        functools.partial(kernel, plan),
        out_shape=(
            jax.ShapeDtypeStruct((R, C), F32),
            jax.ShapeDtypeStruct((R, C), F32),
            jax.ShapeDtypeStruct((R, C), F32),
            jax.ShapeDtypeStruct((n_out * R, C), BF16),
            jax.ShapeDtypeStruct((next_rows, C), BF16),
        ),
        in_specs=[any_spec] * 6,
        out_specs=(any_spec,) * 4 + (pl.BlockSpec(memory_space=pltpu.VMEM),),
        scratch_shapes=[
            pltpu.VMEM((2, B, tokens, R), BF16),
            pltpu.VMEM((tokens, C), BF16),
            pltpu.VMEM((next_rows, width), BF16),
        ]
        + [pltpu.VMEM((R, C), F32)] * 6
        + [
            pltpu.VMEM((C, tokens), BF16),
            pltpu.VMEM((B, C, R), BF16),
            pltpu.VMEM((B, C, R), BF16),
            pltpu.VMEM((B, C, R), BF16),
            pltpu.VMEM((C, R), F32),
            pltpu.VMEM((2, B, R, C), BF16),
            pltpu.VMEM((next_rows, C), F32),
        ]
        + arrived
        + [
            dma((2, B)),
            dma((B,)),
            dma((B,)),
            dma((n_sum, B)),
            dma((n_sum, B)),
            dma((n_keep, B)),
            dma((n_keep, B)),
            dma((n_keep, B)),
            dma((n_keep, B)),
            dma((8 + n_out,)),
        ],
        compiler_params=pltpu.CompilerParams(
            collective_id=0, has_side_effects=True, vmem_limit_bytes=58 * 2**20
        ),
        cost_estimate=pl.CostEstimate(
            flops=2 * (tokens + next_rows) * width * C,
            bytes_accessed=2 * (tokens + next_rows) * width + 24 * R * C,
            transcendentals=R * C,
        ),
    )(activations, output_grads, master_weights, first_moment, second_moment, next_tokens)
    return hand_on(results)


def copy_kernel(*refs):
    count = len(refs) // 2
    copies = [
        pltpu.make_async_copy(refs[i], refs[count + i], refs[-1].at[i]) for i in range(count)
    ]
    for copy in copies:
        copy.start()
    for copy in copies:
        copy.wait()


def hand_on(arrays):
    any_spec = pl.BlockSpec(memory_space=pl.ANY)
    return pl.pallas_call(
        copy_kernel,
        out_shape=tuple(jax.ShapeDtypeStruct(a.shape, a.dtype) for a in arrays),
        in_specs=[any_spec] * len(arrays),
        out_specs=(any_spec,) * len(arrays),
        scratch_shapes=[pltpu.SemaphoreType.DMA((len(arrays),))],
    )(*arrays)


def fits_kernel(mesh):
    n_out, n_in = mesh.shape["outer"], mesh.shape["inner"]
    powers = n_out & (n_out - 1) == 0 and n_in & (n_in - 1) == 0
    return powers and n_out >= 2 and n_in >= 4 and n_out * n_in <= 32


def solution(mesh):
    placed = (
        P(("outer", "inner"), None),
        P(("outer", "inner"), None),
        P(("inner", "outer"), None),
        P(("inner", "outer"), None),
        P(("inner", "outer"), None),
        P(("outer", "inner"), None),
    )
    return jax.shard_map(
        local_kernel if fits_kernel(mesh) else local_plain,
        mesh=mesh,
        in_specs=placed,
        out_specs=(
            P(("inner", "outer"), None),
            P(("inner", "outer"), None),
            P(("inner", "outer"), None),
            P("inner", None),
            P(("outer", "inner"), None),
        ),
        check_vma=False,
    )
```

```python
import functools

import jax
import jax.numpy as jnp
from jax import lax
from jax.experimental import pallas as pl
from jax.experimental.pallas import tpu as pltpu
from jax.sharding import PartitionSpec as P

ADAM_STEP = 10
MESH = pl.DeviceIdType.MESH
BF16 = jnp.bfloat16
F32 = jnp.float32


beta_first = 0.9
beta_second = 0.95
learn_rate = 0.002
decay_rate = 0.1
adam_eps = 1e-08


def adamw_update(gradient, master_weights, first_moment, second_moment):
    new_first = beta_first * first_moment + (1.0 - beta_first) * gradient
    new_second = beta_second * second_moment + (1.0 - beta_second) * gradient * gradient
    first_hat = new_first / (1.0 - beta_first**ADAM_STEP)
    second_hat = new_second / (1.0 - beta_second**ADAM_STEP)
    new_master = master_weights - learn_rate * (
        first_hat / (jnp.sqrt(second_hat) + adam_eps) + decay_rate * master_weights
    )
    return (new_master, new_first, new_second)


def rounded_term(columns, output_grads):
    contrib = jnp.einsum(
        "tr,tc->rc", columns, output_grads, preferred_element_type=jnp.float32
    ).astype(jnp.bfloat16)
    contrib = lax.optimization_barrier(contrib)
    return contrib.astype(jnp.float32)


def regroup_features(activations, outer_count, inner_count):
    tok_rows, width = activations.shape
    shard_rows = width // (outer_count * inner_count)
    split_view = activations.reshape(tok_rows, inner_count, outer_count, shard_rows)
    return split_view.transpose(0, 2, 1, 3).reshape(tok_rows, width)


def local_plain(activations, output_grads, master_weights, first_moment, second_moment, next_tokens):
    outer_count = lax.axis_size("outer")
    inner_count = lax.axis_size("inner")
    regrouped = regroup_features(activations, outer_count, inner_count)
    gradient = lax.psum_scatter(
        rounded_term(regrouped, output_grads), ("outer", "inner"), scatter_dimension=0, tiled=True
    )
    new_master, new_first, new_second = adamw_update(
        gradient, master_weights, first_moment, second_moment
    )
    kept_shard = new_master.astype(jnp.bfloat16)
    kept_weights = lax.all_gather(kept_shard, "outer", axis=0, tiled=True)
    projected = jnp.dot(
        next_tokens,
        lax.all_gather(kept_weights, "inner", axis=0, tiled=True),
        preferred_element_type=jnp.float32,
    )
    return (new_master, new_first, new_second, kept_weights, projected.astype(jnp.bfloat16))


SUM_ORDERS = [((3, 0, 2, 1), 1), ((2, 1, 3, 0), 1)]
GATHER_ORDERS = [((3, 1, 2, 0), 1), ((2, 0, 3, 1), 1)]


class Plan:
    def __init__(self, n_out, n_in, rows, cols):
        self.n_out, self.n_in, self.rows, self.cols = n_out, n_in, rows, cols
        out_bits = [("outer", k) for k in range(n_out.bit_length() - 1)]
        in_bits = [("inner", k) for k in range(1, n_in.bit_length() - 1)]
        ranked = []
        for k in range(max(len(out_bits), len(in_bits))):
            ranked += out_bits[k : k + 1] + in_bits[k : k + 1]
        self.dims = ranked[::-1]
        self.depth = len(ranked)
        self.blocks = 2**self.depth
        self.sum_parts = self.cut(cols, SUM_ORDERS)
        self.keep_parts = self.cut(rows, GATHER_ORDERS)

    def cut(self, extent, orders):
        plain = tuple(range(self.depth - 1, -1, -1))
        share = sum(weight for _, weight in orders)
        parts, lo = [], 0
        for order, weight in orders:
            count = extent * weight // share
            parts.append((order if self.depth == len(order) else plain, lo, count))
            lo += count
        return parts

    def canon(self, order, k):
        return sum(((k >> t) & 1) << order[self.depth - 1 - t] for t in range(self.depth))


def kernel(plan, *refs):
    (act_h, grad_h, mw_h, m1_h, m2_h, nt_h, nm_o, n1_o, n2_o, kept_o, proj_o) = refs[:11]
    (act, grad, nt, mw, m1, m2, nm, n1, n2, grad_t, own, snd0, rcv0, total, weights, acc) = refs[11:27]
    depth, blocks = plan.depth, plan.blocks
    sum_parts, keep_parts = plan.sum_parts, plan.keep_parts
    rv_flat = refs[27 : 27 + len(sum_parts) * depth]
    (
        load_sem,
        core_send,
        core_recv,
        rs_send,
        rs_recv,
        ag_send,
        ag_recv,
        cg_send,
        cg_recv,
        local,
    ) = refs[27 + len(sum_parts) * depth :]
    rv = [rv_flat[p * depth : (p + 1) * depth] for p in range(len(sum_parts))]
    R, C = plan.rows, plan.cols

    outer, inner = lax.axis_index("outer"), lax.axis_index("inner")
    place = {"outer": outer, "inner": inner}

    def bit(axis, k):
        return (place[axis] // 2**k) % 2

    def partner(axis, k):
        other = place[axis] + (1 - 2 * bit(axis, k)) * 2**k
        return (other, inner) if axis == "outer" else (outer, other)

    sibling = partner("inner", 0)
    others = [partner(axis, k) for axis, k in plan.dims]

    barrier = pltpu.get_barrier_semaphore()
    for device in [sibling] + others:
        pl.semaphore_signal(barrier, inc=1, device_id=device, device_id_type=MESH)

    def block_at(flip_core, c):
        o, n = outer, inner
        if flip_core:
            n = n + 1 - 2 * bit("inner", 0)
        for j, (axis, k) in enumerate(plan.dims):
            step = ((c // 2**j) % 2) * (1 - 2 * bit(axis, k)) * 2**k
            if axis == "outer":
                o = o + step
            else:
                n = n + step
        return o, n

    def columns(flip_core, c):
        o, n = block_at(flip_core, c)
        return pl.ds(pl.multiple_of((n * plan.n_out + o) * R, R), R)

    sequence = []
    for k in range(blocks - 1, -1, -1):
        for order, _, _ in sum_parts:
            c = plan.canon(order, k)
            if k >= blocks // 2 and c not in sequence:
                sequence.append(c)
    sequence += [c for c in range(blocks - 1, -1, -1) if c not in sequence]

    first_load = pltpu.make_async_copy(grad_h, grad, local.at[0])
    first_load.start()
    act_loads = {}
    for c in sequence:
        for side in (1, 0):
            load = pltpu.make_async_copy(
                act_h.at[:, columns(side == 1, c)], act.at[side, c], load_sem.at[side, c]
            )
            load.start()
            act_loads[(side, c)] = load
    loads = [
        pltpu.make_async_copy(s, d, local.at[1 + i])
        for i, (s, d) in enumerate([(mw_h, mw), (m1_h, m1), (m2_h, m2), (nt_h, nt)])
    ]
    for load in loads:
        load.start()

    first_load.wait()
    grad_t[...] = grad[...].astype(F32).T.astype(BF16)

    cores = {}

    def term(side, c):
        act_loads[(side, c)].wait()
        return jnp.dot(grad_t[...], act[side, c], preferred_element_type=F32).astype(BF16)

    def send_term(c):
        snd0[c] = term(1, c)
        copy = pltpu.make_async_remote_copy(
            src_ref=snd0.at[c],
            dst_ref=rcv0.at[c],
            send_sem=core_send.at[c],
            recv_sem=core_recv.at[c],
            device_id=sibling,
            device_id_type=MESH,
        )
        copy.start()
        cores[c] = copy

    sums = {}
    arrived = set()
    tile = 64

    def gather_terms(p, k, steps, dst):
        order, lo, count = sum_parts[p]
        c = plan.canon(order, k)
        if c not in arrived:
            arrived.add(c)
            cores[c].wait_recv()
        for t in range(steps):
            sums[(p, k + 2 ** (depth - 1 - t))].wait_recv()

        @pl.loop(0, count // tile)
        def _(i):
            at = pl.multiple_of(i * tile, tile)
            span = pl.ds(lo + at, tile)
            value = own[c, span, :].astype(F32) + rcv0[c, span, :].astype(F32)
            for t in range(steps):
                value += rv[p][t][k, pl.ds(at, tile), :].astype(F32)
            if dst is None:
                own[c, span, :] = value.astype(BF16)
            else:
                dst[span, :] = value

    def send_sum(p, k):
        order, lo, count = sum_parts[p]
        high = k.bit_length() - 1
        step = depth - 1 - high
        gather_terms(p, k, step, None)
        copy = pltpu.make_async_remote_copy(
            src_ref=own.at[plan.canon(order, k), pl.ds(lo, count)],
            dst_ref=rv[p][step].at[k - 2**high],
            send_sem=rs_send.at[p, k],
            recv_sem=rs_recv.at[p, k],
            device_id=others[order[step]],
            device_id_type=MESH,
        )
        copy.start()
        sums[(p, k)] = copy

    pl.semaphore_wait(barrier, 1 + depth)
    lag = 2
    for n in range(blocks + lag):
        if n < blocks:
            c = sequence[n]
            send_term(c)
            own[c] = term(0, c)
        if n >= lag:
            for p, (order, _, _) in enumerate(sum_parts):
                for k in range(blocks - 1, blocks // 2 - 1, -1):
                    if plan.canon(order, k) == sequence[n - lag]:
                        send_sum(p, k)
    for k in range(blocks // 2 - 1, 0, -1):
        for p in range(len(sum_parts)):
            send_sum(p, k)
    for p in range(len(sum_parts)):
        gather_terms(p, 0, depth, total)

    def update(lo, count):
        gradient = total[:, lo : lo + count].T
        span = pl.ds(lo, count)
        master, first, second = adamw_update(gradient, mw[span, :], m1[span, :], m2[span, :])
        nm[span, :] = master
        n1[span, :] = first
        n2[span, :] = second
        weights[0, 0, span, :] = master.astype(BF16)

    for load in loads[:3]:
        load.wait()

    def project(side, c):
        acc[...] += jnp.dot(
            nt[:, columns(side == 1, c)], weights[side, c], preferred_element_type=F32
        )

    passed, crossed, keeps = {}, {}, []
    have = {c: 0 for c in range(blocks)}
    inner_mask = sum(2**j for j, (axis, _) in enumerate(plan.dims) if axis == "inner")
    pending = []

    def finish_sibling(c):
        for p in range(len(keep_parts)):
            crossed[(p, c)].wait_recv()
        project(1, c)

    for q in range(blocks):
        ready = []
        for p, (order, lo, count) in enumerate(keep_parts):
            c = plan.canon(order, q)
            if q == 0:
                update(lo, count)
            high = q.bit_length() - 1
            if q > 0:
                passed[(p, q - 2**high, high)].wait_recv()
            rows = pl.ds(lo, count)
            for t in range(high + 1, depth):
                e = order[depth - 1 - t]
                copy = pltpu.make_async_remote_copy(
                    src_ref=weights.at[0, c, rows],
                    dst_ref=weights.at[0, c + 2**e, rows],
                    send_sem=ag_send.at[p, q + 2**t],
                    recv_sem=ag_recv.at[p, q + 2**t],
                    device_id=others[e],
                    device_id_type=MESH,
                )
                copy.start()
                passed[(p, q, t)] = copy
            copy = pltpu.make_async_remote_copy(
                src_ref=weights.at[0, c, rows],
                dst_ref=weights.at[1, c, rows],
                send_sem=cg_send.at[p, c],
                recv_sem=cg_recv.at[p, c],
                device_id=sibling,
                device_id_type=MESH,
            )
            copy.start()
            crossed[(p, c)] = copy
            have[c] += 1
            if have[c] == len(keep_parts):
                ready.append(c)
        if q == 0:
            stores = [
                pltpu.make_async_copy(s, d, local.at[5 + i])
                for i, (s, d) in enumerate([(nm, nm_o), (n1, n1_o), (n2, n2_o)])
            ]
            for store in stores:
                store.start()
            acc[...] = jnp.zeros_like(acc)
            loads[3].wait()
        for c in ready:
            if c & inner_mask == 0:
                o, _ = block_at(False, c)
                keep = pltpu.make_async_copy(
                    weights.at[0, c],
                    kept_o.at[pl.ds(pl.multiple_of(o * R, R), R)],
                    local.at[8 + len(keeps)],
                )
                keep.start()
                keeps.append(keep)
            project(0, c)
            pending.append(c)
        while len(pending) > 2:
            finish_sibling(pending.pop(0))
    for c in pending:
        finish_sibling(c)
    proj_o[...] = acc[...].astype(BF16)

    for copy in list(cores.values()) + list(sums.values()) + list(passed.values()) + list(crossed.values()):
        copy.wait_send()
    for copy in stores + keeps:
        copy.wait()


def local_kernel(activations, output_grads, master_weights, first_moment, second_moment, next_tokens):
    n_out, n_in = lax.axis_size("outer"), lax.axis_size("inner")
    tokens, width = activations.shape
    next_rows = next_tokens.shape[0]
    R, C = master_weights.shape
    plan = Plan(n_out, n_in, R, C)
    B, L = plan.blocks, plan.depth
    n_sum, n_keep = len(plan.sum_parts), len(plan.keep_parts)
    dma = pltpu.SemaphoreType.DMA
    any_spec = pl.BlockSpec(memory_space=pl.ANY)
    arrived = [
        pltpu.VMEM((2 ** (L - 1 - s), count, R), BF16)
        for _, _, count in plan.sum_parts
        for s in range(L)
    ]
    results = pl.pallas_call(
        functools.partial(kernel, plan),
        out_shape=(
            jax.ShapeDtypeStruct((R, C), F32),
            jax.ShapeDtypeStruct((R, C), F32),
            jax.ShapeDtypeStruct((R, C), F32),
            jax.ShapeDtypeStruct((n_out * R, C), BF16),
            jax.ShapeDtypeStruct((next_rows, C), BF16),
        ),
        in_specs=[any_spec] * 6,
        out_specs=(any_spec,) * 4 + (pl.BlockSpec(memory_space=pltpu.VMEM),),
        scratch_shapes=[
            pltpu.VMEM((2, B, tokens, R), BF16),
            pltpu.VMEM((tokens, C), BF16),
            pltpu.VMEM((next_rows, width), BF16),
        ]
        + [pltpu.VMEM((R, C), F32)] * 6
        + [
            pltpu.VMEM((C, tokens), BF16),
            pltpu.VMEM((B, C, R), BF16),
            pltpu.VMEM((B, C, R), BF16),
            pltpu.VMEM((B, C, R), BF16),
            pltpu.VMEM((C, R), F32),
            pltpu.VMEM((2, B, R, C), BF16),
            pltpu.VMEM((next_rows, C), F32),
        ]
        + arrived
        + [
            dma((2, B)),
            dma((B,)),
            dma((B,)),
            dma((n_sum, B)),
            dma((n_sum, B)),
            dma((n_keep, B)),
            dma((n_keep, B)),
            dma((n_keep, B)),
            dma((n_keep, B)),
            dma((8 + n_out,)),
        ],
        compiler_params=pltpu.CompilerParams(
            collective_id=0, has_side_effects=True, vmem_limit_bytes=58 * 2**20
        ),
        cost_estimate=pl.CostEstimate(
            flops=2 * (tokens + next_rows) * width * C,
            bytes_accessed=2 * (tokens + next_rows) * width + 24 * R * C,
            transcendentals=R * C,
        ),
    )(activations, output_grads, master_weights, first_moment, second_moment, next_tokens)
    return hand_on(results)


def copy_kernel(pieces, *refs):
    count = len(refs) // 3
    sources, targets, held, sems = refs[:count], refs[count : 2 * count], refs[2 * count : -1], refs[-1]
    spans = [
        (i, pl.ds(n * (ref.shape[0] // pieces), ref.shape[0] // pieces))
        for i, ref in enumerate(sources)
        for n in range(pieces)
    ]
    ins = [
        pltpu.make_async_copy(sources[i].at[at], held[i].at[at], sems.at[0, n])
        for n, (i, at) in enumerate(spans)
    ]
    outs = [
        pltpu.make_async_copy(held[i].at[at], targets[i].at[at], sems.at[1, n])
        for n, (i, at) in enumerate(spans)
    ]
    for copy in ins:
        copy.start()
    for copy, onward in zip(ins, outs):
        copy.wait()
        onward.start()
    for copy in outs:
        copy.wait()


def hand_on(arrays, pieces=2):
    any_spec = pl.BlockSpec(memory_space=pl.ANY)
    return pl.pallas_call(
        functools.partial(copy_kernel, pieces),
        out_shape=tuple(jax.ShapeDtypeStruct(a.shape, a.dtype) for a in arrays),
        in_specs=[any_spec] * len(arrays),
        out_specs=(any_spec,) * len(arrays),
        scratch_shapes=[pltpu.VMEM(a.shape, a.dtype) for a in arrays]
        + [pltpu.SemaphoreType.DMA((2, pieces * len(arrays)))],
        compiler_params=pltpu.CompilerParams(vmem_limit_bytes=48 * 2**20),
    )(*arrays)


def fits_kernel(mesh):
    n_out, n_in = mesh.shape["outer"], mesh.shape["inner"]
    powers = n_out & (n_out - 1) == 0 and n_in & (n_in - 1) == 0
    return powers and n_out >= 2 and n_in >= 4 and n_out * n_in <= 32


def solution(mesh):
    placed = (
        P(("outer", "inner"), None),
        P(("outer", "inner"), None),
        P(("inner", "outer"), None),
        P(("inner", "outer"), None),
        P(("inner", "outer"), None),
        P(("outer", "inner"), None),
    )
    return jax.shard_map(
        local_kernel if fits_kernel(mesh) else local_plain,
        mesh=mesh,
        in_specs=placed,
        out_specs=(
            P(("inner", "outer"), None),
            P(("inner", "outer"), None),
            P(("inner", "outer"), None),
            P("inner", None),
            P(("outer", "inner"), None),
        ),
        check_vma=False,
    )
```

```python
import functools

import jax
import jax.numpy as jnp
from jax import lax
from jax.experimental import pallas as pl
from jax.experimental.pallas import tpu as pltpu
from jax.sharding import PartitionSpec as P

ADAM_STEP = 10
MESH = pl.DeviceIdType.MESH
BF16 = jnp.bfloat16
F32 = jnp.float32


beta_first = 0.9
beta_second = 0.95
learn_rate = 0.002
decay_rate = 0.1
adam_eps = 1e-08


def adamw_update(gradient, master_weights, first_moment, second_moment):
    new_first = beta_first * first_moment + (1.0 - beta_first) * gradient
    new_second = beta_second * second_moment + (1.0 - beta_second) * gradient * gradient
    first_hat = new_first / (1.0 - beta_first**ADAM_STEP)
    second_hat = new_second / (1.0 - beta_second**ADAM_STEP)
    new_master = master_weights - learn_rate * (
        first_hat / (jnp.sqrt(second_hat) + adam_eps) + decay_rate * master_weights
    )
    return (new_master, new_first, new_second)


def rounded_term(columns, output_grads):
    contrib = jnp.einsum(
        "tr,tc->rc", columns, output_grads, preferred_element_type=jnp.float32
    ).astype(jnp.bfloat16)
    contrib = lax.optimization_barrier(contrib)
    return contrib.astype(jnp.float32)


def regroup_features(activations, outer_count, inner_count):
    tok_rows, width = activations.shape
    shard_rows = width // (outer_count * inner_count)
    split_view = activations.reshape(tok_rows, inner_count, outer_count, shard_rows)
    return split_view.transpose(0, 2, 1, 3).reshape(tok_rows, width)


def local_plain(activations, output_grads, master_weights, first_moment, second_moment, next_tokens):
    outer_count = lax.axis_size("outer")
    inner_count = lax.axis_size("inner")
    regrouped = regroup_features(activations, outer_count, inner_count)
    gradient = lax.psum_scatter(
        rounded_term(regrouped, output_grads), ("outer", "inner"), scatter_dimension=0, tiled=True
    )
    new_master, new_first, new_second = adamw_update(
        gradient, master_weights, first_moment, second_moment
    )
    kept_shard = new_master.astype(jnp.bfloat16)
    kept_weights = lax.all_gather(kept_shard, "outer", axis=0, tiled=True)
    projected = jnp.dot(
        next_tokens,
        lax.all_gather(kept_weights, "inner", axis=0, tiled=True),
        preferred_element_type=jnp.float32,
    )
    return (new_master, new_first, new_second, kept_weights, projected.astype(jnp.bfloat16))


SUM_ORDERS = [
    [(3, 2, 1, 0), (2, 3, 1, 0)],
    [(3, 2, 1, 0), (2, 3, 1, 0)],
]
GATHER_ORDERS = [
    [(3, 2, 1, 0), (2, 3, 1, 0)],
    [(3, 2, 1, 0), (2, 3, 1, 0)],
]
STEPS = [
    ("T", 0, 15), ("T", 0, 14), ("T", 0, 13), ("T", 0, 12), ("T", 0, 11), ("S", 0, 0, 15),
    ("S", 0, 1, 15), ("S", 0, 0, 14), ("S", 0, 1, 14), ("S", 0, 0, 13), ("S", 0, 1, 13),
    ("S", 0, 0, 12), ("S", 0, 1, 12), ("T", 0, 7), ("S", 0, 0, 11), ("T", 0, 10), ("T", 0, 6),
    ("T", 0, 9), ("S", 0, 1, 11), ("S", 0, 0, 7), ("S", 0, 1, 7), ("T", 0, 5), ("S", 0, 0, 10),
    ("S", 0, 1, 10), ("S", 0, 0, 6), ("S", 0, 0, 9), ("S", 0, 1, 6), ("T", 0, 8), ("T", 0, 4),
    ("S", 0, 1, 9), ("S", 0, 0, 5), ("S", 0, 1, 5), ("T", 0, 3), ("T", 0, 2), ("S", 0, 0, 8),
    ("S", 0, 1, 8), ("S", 0, 0, 4), ("S", 0, 1, 4), ("T", 0, 1), ("T", 0, 0), ("T", 1, 15),
    ("T", 1, 14), ("T", 1, 13), ("S", 0, 0, 3), ("S", 0, 1, 3), ("T", 1, 12), ("S", 1, 0, 15),
    ("S", 1, 1, 15), ("S", 1, 0, 14), ("S", 1, 1, 14), ("S", 1, 0, 13), ("S", 1, 1, 13),
    ("T", 1, 11), ("S", 1, 0, 12), ("S", 1, 1, 12), ("T", 1, 7), ("S", 0, 0, 2), ("T", 1, 10),
    ("T", 1, 6), ("S", 1, 0, 11), ("S", 0, 1, 2), ("T", 1, 9), ("S", 1, 1, 11), ("T", 1, 5),
    ("S", 1, 0, 10), ("S", 1, 1, 10), ("S", 0, 1, 1), ("S", 0, 0, 1), ("T", 1, 8), ("S", 1, 0, 9),
    ("T", 1, 4), ("S", 1, 1, 9), ("T", 1, 3), ("T", 1, 2), ("S", 1, 0, 8), ("T", 1, 1),
    ("S", 1, 1, 8), ("T", 1, 0), ("S", 1, 0, 7), ("S", 1, 1, 7), ("S", 1, 0, 6), ("S", 1, 1, 6),
    ("F", 0), ("A", 0, 0, 0), ("A", 0, 1, 0), ("S", 1, 0, 5), ("S", 1, 1, 5), ("S", 1, 0, 4),
    ("S", 1, 1, 4), ("D", 0, 0, 0), ("A", 0, 0, 1), ("D", 1, 0, 0), ("A", 0, 0, 2),
    ("A", 0, 1, 2), ("D", 0, 0, 2), ("A", 0, 1, 1), ("D", 0, 0, 1), ("D", 1, 0, 2),
    ("S", 1, 1, 3), ("S", 1, 0, 3), ("D", 1, 0, 1), ("S", 1, 1, 2), ("S", 1, 0, 2),
    ("A", 0, 0, 3), ("A", 0, 0, 8), ("A", 0, 0, 4), ("A", 0, 1, 4), ("A", 0, 1, 8),
    ("D", 0, 0, 4), ("D", 0, 0, 8), ("D", 1, 0, 8), ("S", 1, 1, 1), ("A", 0, 1, 3),
    ("S", 1, 0, 1), ("D", 0, 0, 3), ("D", 1, 0, 4), ("D", 1, 0, 3), ("A", 0, 0, 9),
    ("A", 0, 0, 5), ("A", 0, 0, 10), ("A", 0, 0, 6), ("A", 0, 1, 6), ("A", 0, 1, 10),
    ("D", 0, 0, 6), ("D", 0, 0, 10), ("F", 1), ("A", 0, 1, 5), ("A", 0, 0, 7), ("A", 0, 1, 9),
    ("A", 0, 0, 11), ("A", 1, 0, 0), ("A", 1, 1, 0), ("A", 0, 0, 12), ("A", 0, 1, 12),
    ("D", 0, 0, 5), ("D", 1, 0, 5), ("D", 1, 0, 6), ("D", 0, 0, 9), ("D", 1, 0, 9),
    ("D", 1, 0, 10), ("D", 0, 0, 12), ("A", 0, 1, 7), ("A", 0, 1, 11), ("D", 0, 0, 7),
    ("D", 0, 0, 11), ("D", 1, 0, 12), ("D", 0, 1, 0), ("D", 1, 1, 0), ("A", 1, 0, 2),
    ("A", 0, 0, 13), ("D", 1, 0, 11), ("A", 0, 1, 14), ("A", 1, 0, 1), ("D", 1, 0, 7),
    ("A", 0, 0, 14), ("D", 0, 0, 14), ("A", 0, 1, 13), ("D", 0, 0, 13), ("A", 1, 1, 2),
    ("D", 0, 1, 2), ("D", 1, 0, 14), ("A", 0, 0, 15), ("A", 1, 0, 4), ("A", 1, 1, 1),
    ("D", 1, 0, 13), ("D", 0, 1, 1), ("D", 1, 1, 2), ("A", 1, 0, 8), ("A", 1, 1, 8),
    ("D", 0, 1, 4), ("D", 1, 1, 1), ("A", 1, 0, 3), ("A", 1, 1, 4), ("A", 0, 1, 15),
    ("D", 0, 0, 15), ("D", 1, 1, 4), ("D", 0, 1, 8), ("A", 1, 1, 3), ("D", 0, 1, 3),
    ("D", 1, 1, 8), ("A", 1, 0, 10), ("A", 1, 0, 6), ("D", 1, 0, 15), ("D", 1, 1, 3),
    ("A", 1, 0, 9), ("A", 1, 0, 5), ("A", 1, 1, 6), ("A", 1, 1, 10), ("D", 0, 1, 6),
    ("D", 0, 1, 10), ("D", 1, 1, 10), ("A", 1, 0, 12), ("A", 1, 1, 9), ("D", 0, 1, 5),
    ("D", 1, 1, 6), ("A", 1, 1, 5), ("A", 1, 0, 7), ("D", 1, 1, 5), ("D", 0, 1, 9),
    ("D", 1, 1, 9), ("A", 1, 0, 11), ("A", 1, 1, 12), ("D", 0, 1, 12), ("A", 1, 1, 7),
    ("A", 1, 1, 11), ("D", 0, 1, 7), ("D", 0, 1, 11), ("D", 1, 1, 12), ("D", 1, 1, 11),
    ("A", 1, 0, 14), ("A", 1, 1, 14), ("D", 1, 1, 7), ("D", 0, 1, 14), ("A", 1, 0, 13),
    ("A", 1, 1, 13), ("D", 0, 1, 13), ("D", 1, 1, 14), ("A", 1, 0, 15), ("D", 1, 1, 13),
    ("A", 1, 1, 15), ("D", 0, 1, 15), ("D", 1, 1, 15),
]


class Plan:
    def __init__(self, n_out, n_in, rows, cols):
        self.n_out, self.n_in, self.rows, self.cols = n_out, n_in, rows, cols
        out_bits = [("outer", k) for k in range(n_out.bit_length() - 1)]
        in_bits = [("inner", k) for k in range(1, n_in.bit_length() - 1)]
        ranked = []
        for k in range(max(len(out_bits), len(in_bits))):
            ranked += out_bits[k : k + 1] + in_bits[k : k + 1]
        self.dims = ranked[::-1]
        self.depth = len(ranked)
        self.blocks = 2**self.depth
        self.groups = len(SUM_ORDERS)
        self.parts = len(SUM_ORDERS[0])
        self.group_cols = cols // self.groups

    def canon(self, order, k):
        return sum(((k >> t) & 1) << order[self.depth - 1 - t] for t in range(self.depth))


def kernel(plan, *refs):
    (act_h, grad_h, mw_h, m1_h, m2_h, nt_h, nm_o, n1_o, n2_o, kept_o, proj_o) = refs[:11]
    (act, grad, nt, mw, m1, m2, nm, n1, n2, grad_t, own, snd0, rcv0, total, weights, acc) = refs[11:27]
    depth, blocks, groups, parts = plan.depth, plan.blocks, plan.groups, plan.parts
    rv_flat = refs[27 : 27 + groups * parts * depth]
    (
        load_sem,
        core_send,
        core_recv,
        rs_send,
        rs_recv,
        ag_send,
        ag_recv,
        cg_send,
        cg_recv,
        local,
        group_local,
    ) = refs[27 + groups * parts * depth :]
    rv = {
        (g, p): rv_flat[(g * parts + p) * depth : (g * parts + p + 1) * depth]
        for g in range(groups)
        for p in range(parts)
    }
    wide = plan.group_cols
    R, C = plan.rows, plan.cols

    outer, inner = lax.axis_index("outer"), lax.axis_index("inner")
    place = {"outer": outer, "inner": inner}

    def bit(axis, k):
        return (place[axis] // 2**k) % 2

    def partner(axis, k):
        other = place[axis] + (1 - 2 * bit(axis, k)) * 2**k
        return (other, inner) if axis == "outer" else (outer, other)

    sibling = partner("inner", 0)
    others = [partner(axis, k) for axis, k in plan.dims]

    barrier = pltpu.get_barrier_semaphore()
    for device in [sibling] + others:
        pl.semaphore_signal(barrier, inc=1, device_id=device, device_id_type=MESH)

    def block_at(flip_core, c):
        o, n = outer, inner
        if flip_core:
            n = n + 1 - 2 * bit("inner", 0)
        for j, (axis, k) in enumerate(plan.dims):
            step = ((c // 2**j) % 2) * (1 - 2 * bit(axis, k)) * 2**k
            if axis == "outer":
                o = o + step
            else:
                n = n + step
        return o, n

    def columns(flip_core, c):
        o, n = block_at(flip_core, c)
        return pl.ds(pl.multiple_of((n * plan.n_out + o) * R, R), R)

    sequence = [step[2] for step in STEPS if step[0] == "T" and step[1] == 0]

    first_load = pltpu.make_async_copy(grad_h, grad, local.at[0])
    first_load.start()
    act_loads = {}
    for c in sequence:
        for side in (1, 0):
            load = pltpu.make_async_copy(
                act_h.at[:, columns(side == 1, c)], act.at[side, c], load_sem.at[side, c]
            )
            load.start()
            act_loads[(side, c)] = load
    loads = [
        pltpu.make_async_copy(s, d, local.at[1 + i])
        for i, (s, d) in enumerate([(mw_h, mw), (m1_h, m1), (m2_h, m2), (nt_h, nt)])
    ]
    for load in loads:
        load.start()

    first_load.wait()
    grad_t[...] = grad[...].astype(F32).T.astype(BF16)
    pl.semaphore_wait(barrier, 1 + depth)

    cores, sums, passed, crossed, stores = {}, {}, {}, {}, []
    done = set()

    def once(key, wait):
        if key not in done:
            done.add(key)
            wait()

    def group_span(g):
        return pl.ds(g * wide, wide)

    def term(side, g, c):
        once(("act", side, c), act_loads[(side, c)].wait)
        return jnp.dot(
            grad_t[group_span(g), :], act[side, c], preferred_element_type=F32
        ).astype(BF16)

    def send_term(g, c):
        at = (c, group_span(g))
        snd0[c, group_span(g), :] = term(1, g, c)
        copy = pltpu.make_async_remote_copy(
            src_ref=snd0.at[at],
            dst_ref=rcv0.at[at],
            send_sem=core_send.at[g, c],
            recv_sem=core_recv.at[g, c],
            device_id=sibling,
            device_id_type=MESH,
        )
        copy.start()
        cores[(g, c)] = copy
        own[c, group_span(g), :] = term(0, g, c)

    count = wide // parts
    tile = min(count, 64)

    def gather_terms(g, p, k, steps, last):
        c = plan.canon(SUM_ORDERS[g][p], k)
        once(("core", g, c), cores[(g, c)].wait_recv)
        for t in range(steps):
            sums[(g, p, k + 2 ** (depth - 1 - t))].wait_recv()
        for at in range(0, count, tile):
            span = pl.ds(g * wide + p * count + at, tile)
            value = own[c, span, :].astype(F32) + rcv0[c, span, :].astype(F32)
            for t in range(steps):
                value += rv[(g, p)][t][k, pl.ds(at, tile), :].astype(F32)
            if last:
                total[span, :] = value
            else:
                own[c, span, :] = value.astype(BF16)

    def send_sum(g, p, k):
        order = SUM_ORDERS[g][p]
        high = k.bit_length() - 1
        step = depth - 1 - high
        gather_terms(g, p, k, step, False)
        copy = pltpu.make_async_remote_copy(
            src_ref=own.at[plan.canon(order, k), pl.ds(g * wide + p * count, count)],
            dst_ref=rv[(g, p)][step].at[k - 2**high],
            send_sem=rs_send.at[g * parts + p, k],
            recv_sem=rs_recv.at[g * parts + p, k],
            device_id=others[order[step]],
            device_id_type=MESH,
        )
        copy.start()
        sums[(g, p, k)] = copy

    def update(g):
        for p in range(parts):
            gather_terms(g, p, 0, depth, True)
        once("state", lambda: [load.wait() for load in loads[:3]])
        span = group_span(g)
        gradient = total[span, :].T
        master, first, second = adamw_update(gradient, mw[:, span], m1[:, span], m2[:, span])
        weights[0, g, 0] = master.astype(BF16)
        nm[:, span] = master
        n1[:, span] = first
        n2[:, span] = second
        for i, (s, d) in enumerate([(nm, nm_o), (n1, n1_o), (n2, n2_o)]):
            store = pltpu.make_async_copy(s.at[:, span], d.at[:, span], group_local.at[g, i])
            store.start()
            stores.append(store)

    def pass_on(g, p, q):
        order = GATHER_ORDERS[g][p]
        c = plan.canon(order, q)
        high = q.bit_length() - 1
        if q > 0:
            passed[(g, p, q)].wait_recv()
        rows = pl.ds(p * (R // parts), R // parts)
        for t in range(high + 1, depth):
            e = order[depth - 1 - t]
            copy = pltpu.make_async_remote_copy(
                src_ref=weights.at[0, g, c, rows],
                dst_ref=weights.at[0, g, c + 2**e, rows],
                send_sem=ag_send.at[g * parts + p, q + 2**t],
                recv_sem=ag_recv.at[g * parts + p, q + 2**t],
                device_id=others[e],
                device_id_type=MESH,
            )
            copy.start()
            passed[(g, p, q + 2**t)] = copy
        copy = pltpu.make_async_remote_copy(
            src_ref=weights.at[0, g, c, rows],
            dst_ref=weights.at[1, g, c, rows],
            send_sem=cg_send.at[g * parts + p, c],
            recv_sem=cg_recv.at[g * parts + p, c],
            device_id=sibling,
            device_id_type=MESH,
        )
        copy.start()
        crossed[(g, p, c)] = copy

    inner_mask = sum(2**j for j, (axis, _) in enumerate(plan.dims) if axis == "inner")

    def project(side, g, c):
        span = group_span(g)
        if side == 1:
            for p in range(parts):
                crossed[(g, p, c)].wait_recv()
        elif c & inner_mask == 0:
            o, _ = block_at(False, c)
            keep = pltpu.make_async_copy(
                weights.at[0, g, c],
                kept_o.at[pl.ds(pl.multiple_of(o * R, R), R), span],
                group_local.at[g, 3 + c],
            )
            keep.start()
            stores.append(keep)
        once("next", loads[3].wait)
        share = jnp.dot(
            nt[:, columns(side == 1, c)], weights[side, g, c], preferred_element_type=F32
        )
        if ("acc", g) in done:
            acc[:, span] += share
        else:
            done.add(("acc", g))
            acc[:, span] = share

    run = {"T": send_term, "S": send_sum, "F": update, "A": pass_on, "D": project}
    for step in STEPS:
        run[step[0]](*step[1:])
    proj_o[...] = acc[...].astype(BF16)

    for group in (cores, sums, passed, crossed):
        for copy in group.values():
            copy.wait_send()
    for copy in stores:
        copy.wait()


def local_kernel(activations, output_grads, master_weights, first_moment, second_moment, next_tokens):
    n_out, n_in = lax.axis_size("outer"), lax.axis_size("inner")
    tokens, width = activations.shape
    next_rows = next_tokens.shape[0]
    R, C = master_weights.shape
    plan = Plan(n_out, n_in, R, C)
    B, L, G, n_parts = plan.blocks, plan.depth, plan.groups, plan.groups * plan.parts
    dma = pltpu.SemaphoreType.DMA
    any_spec = pl.BlockSpec(memory_space=pl.ANY)
    arrived = [
        pltpu.VMEM((2 ** (L - 1 - s), plan.group_cols // plan.parts, R), BF16)
        for _ in range(n_parts)
        for s in range(L)
    ]
    results = pl.pallas_call(
        functools.partial(kernel, plan),
        out_shape=(
            jax.ShapeDtypeStruct((R, C), F32),
            jax.ShapeDtypeStruct((R, C), F32),
            jax.ShapeDtypeStruct((R, C), F32),
            jax.ShapeDtypeStruct((n_out * R, C), BF16),
            jax.ShapeDtypeStruct((next_rows, C), BF16),
        ),
        in_specs=[any_spec] * 6,
        out_specs=(any_spec,) * 4 + (pl.BlockSpec(memory_space=pltpu.VMEM),),
        scratch_shapes=[
            pltpu.VMEM((2, B, tokens, R), BF16),
            pltpu.VMEM((tokens, C), BF16),
            pltpu.VMEM((next_rows, width), BF16),
        ]
        + [pltpu.VMEM((R, C), F32)] * 6
        + [
            pltpu.VMEM((C, tokens), BF16),
            pltpu.VMEM((B, C, R), BF16),
            pltpu.VMEM((B, C, R), BF16),
            pltpu.VMEM((B, C, R), BF16),
            pltpu.VMEM((C, R), F32),
            pltpu.VMEM((2, G, B, R, plan.group_cols), BF16),
            pltpu.VMEM((next_rows, C), F32),
        ]
        + arrived
        + [
            dma((2, B)),
            dma((G, B)),
            dma((G, B)),
            dma((n_parts, B)),
            dma((n_parts, B)),
            dma((n_parts, B)),
            dma((n_parts, B)),
            dma((n_parts, B)),
            dma((n_parts, B)),
            dma((5,)),
            dma((G, 3 + B)),
        ],
        compiler_params=pltpu.CompilerParams(
            collective_id=0, has_side_effects=True, vmem_limit_bytes=58 * 2**20
        ),
        cost_estimate=pl.CostEstimate(
            flops=2 * (tokens + next_rows) * width * C,
            bytes_accessed=2 * (tokens + next_rows) * width + 24 * R * C,
            transcendentals=R * C,
        ),
    )(activations, output_grads, master_weights, first_moment, second_moment, next_tokens)
    return hand_on(results)


def copy_kernel(pieces, *refs):
    count = len(refs) // 3
    sources, targets, held, sems = refs[:count], refs[count : 2 * count], refs[2 * count : -1], refs[-1]
    spans = [
        (i, pl.ds(n * (ref.shape[0] // pieces), ref.shape[0] // pieces))
        for i, ref in enumerate(sources)
        for n in range(pieces)
    ]
    ins = [
        pltpu.make_async_copy(sources[i].at[at], held[i].at[at], sems.at[0, n])
        for n, (i, at) in enumerate(spans)
    ]
    outs = [
        pltpu.make_async_copy(held[i].at[at], targets[i].at[at], sems.at[1, n])
        for n, (i, at) in enumerate(spans)
    ]
    for copy in ins:
        copy.start()
    for copy, onward in zip(ins, outs):
        copy.wait()
        onward.start()
    for copy in outs:
        copy.wait()


def hand_on(arrays, pieces=2):
    any_spec = pl.BlockSpec(memory_space=pl.ANY)
    return pl.pallas_call(
        functools.partial(copy_kernel, pieces),
        out_shape=tuple(jax.ShapeDtypeStruct(a.shape, a.dtype) for a in arrays),
        in_specs=[any_spec] * len(arrays),
        out_specs=(any_spec,) * len(arrays),
        scratch_shapes=[pltpu.VMEM(a.shape, a.dtype) for a in arrays]
        + [pltpu.SemaphoreType.DMA((2, pieces * len(arrays)))],
        compiler_params=pltpu.CompilerParams(vmem_limit_bytes=60 * 2**20),
    )(*arrays)


def fits_kernel(mesh):
    n_out, n_in = mesh.shape["outer"], mesh.shape["inner"]
    return n_out == 8 and n_in == 4


def solution(mesh):
    placed = (
        P(("outer", "inner"), None),
        P(("outer", "inner"), None),
        P(("inner", "outer"), None),
        P(("inner", "outer"), None),
        P(("inner", "outer"), None),
        P(("outer", "inner"), None),
    )
    return jax.shard_map(
        local_kernel if fits_kernel(mesh) else local_plain,
        mesh=mesh,
        in_specs=placed,
        out_specs=(
            P(("inner", "outer"), None),
            P(("inner", "outer"), None),
            P(("inner", "outer"), None),
            P("inner", None),
            P(("outer", "inner"), None),
        ),
        check_vma=False,
    )
```

```python
import functools

import jax
import jax.numpy as jnp
from jax import lax
from jax.experimental import pallas as pl
from jax.experimental.pallas import tpu as pltpu
from jax.sharding import PartitionSpec as P

ADAM_STEP = 10
MESH = pl.DeviceIdType.MESH
BF16 = jnp.bfloat16
F32 = jnp.float32


beta_first = 0.9
beta_second = 0.95
learn_rate = 0.002
decay_rate = 0.1
adam_eps = 1e-08


def adamw_update(gradient, master_weights, first_moment, second_moment):
    new_first = beta_first * first_moment + (1.0 - beta_first) * gradient
    new_second = beta_second * second_moment + (1.0 - beta_second) * gradient * gradient
    first_hat = new_first / (1.0 - beta_first**ADAM_STEP)
    second_hat = new_second / (1.0 - beta_second**ADAM_STEP)
    new_master = master_weights - learn_rate * (
        first_hat / (jnp.sqrt(second_hat) + adam_eps) + decay_rate * master_weights
    )
    return (new_master, new_first, new_second)


def rounded_term(columns, output_grads):
    contrib = jnp.einsum(
        "tr,tc->rc", columns, output_grads, preferred_element_type=jnp.float32
    ).astype(jnp.bfloat16)
    contrib = lax.optimization_barrier(contrib)
    return contrib.astype(jnp.float32)


def regroup_features(activations, outer_count, inner_count):
    tok_rows, width = activations.shape
    shard_rows = width // (outer_count * inner_count)
    split_view = activations.reshape(tok_rows, inner_count, outer_count, shard_rows)
    return split_view.transpose(0, 2, 1, 3).reshape(tok_rows, width)


def local_plain(activations, output_grads, master_weights, first_moment, second_moment, next_tokens):
    outer_count = lax.axis_size("outer")
    inner_count = lax.axis_size("inner")
    regrouped = regroup_features(activations, outer_count, inner_count)
    gradient = lax.psum_scatter(
        rounded_term(regrouped, output_grads), ("outer", "inner"), scatter_dimension=0, tiled=True
    )
    new_master, new_first, new_second = adamw_update(
        gradient, master_weights, first_moment, second_moment
    )
    kept_shard = new_master.astype(jnp.bfloat16)
    kept_weights = lax.all_gather(kept_shard, "outer", axis=0, tiled=True)
    projected = jnp.dot(
        next_tokens,
        lax.all_gather(kept_weights, "inner", axis=0, tiled=True),
        preferred_element_type=jnp.float32,
    )
    return (new_master, new_first, new_second, kept_weights, projected.astype(jnp.bfloat16))


SUM_ORDERS = [
    [(3, 0, 1, 2), (2, 1, 3, 0)],
    [(3, 2, 1, 0), (2, 1, 0, 3)],
]
GATHER_ORDERS = [
    [(2, 3, 0, 1), (3, 2, 1, 0)],
    [(3, 0, 2, 1), (2, 1, 3, 0)],
]
STEPS = [
    ("T", 0, 15), ("T", 0, 11), ("T", 0, 14), ("T", 0, 13), ("T", 0, 7), ("S", 0, 0, 15),
    ("S", 0, 1, 15), ("S", 0, 0, 14), ("T", 0, 9), ("S", 0, 1, 14), ("S", 0, 0, 13),
    ("S", 0, 0, 11), ("S", 0, 1, 13), ("S", 0, 1, 11), ("T", 0, 6), ("T", 0, 10), ("S", 0, 0, 12),
    ("S", 0, 0, 7), ("S", 0, 1, 7), ("T", 0, 12), ("T", 0, 5), ("S", 0, 1, 12), ("S", 0, 0, 10),
    ("T", 0, 8), ("T", 0, 4), ("S", 0, 1, 10), ("S", 0, 0, 9), ("S", 0, 1, 9), ("T", 0, 3),
    ("S", 0, 1, 6), ("S", 0, 0, 8), ("S", 0, 0, 5), ("S", 0, 1, 8), ("T", 0, 2), ("S", 0, 1, 3),
    ("T", 0, 1), ("S", 0, 0, 6), ("S", 0, 1, 5), ("S", 0, 0, 3), ("T", 0, 0), ("T", 1, 15),
    ("T", 1, 14), ("S", 0, 0, 4), ("T", 1, 7), ("S", 0, 1, 4), ("T", 1, 13), ("S", 0, 1, 2),
    ("S", 1, 0, 15), ("S", 1, 1, 15), ("S", 1, 0, 14), ("S", 1, 1, 13), ("S", 1, 1, 14),
    ("T", 1, 12), ("S", 1, 0, 13), ("S", 1, 1, 11), ("T", 1, 6), ("T", 1, 11), ("T", 1, 10),
    ("S", 1, 0, 12), ("S", 1, 1, 9), ("T", 1, 5), ("S", 0, 1, 1), ("S", 1, 1, 12), ("S", 0, 0, 2),
    ("S", 1, 0, 11), ("S", 1, 0, 10), ("S", 1, 1, 7), ("T", 1, 9), ("S", 0, 0, 1),
    ("S", 1, 1, 10), ("T", 1, 8), ("S", 1, 1, 5), ("T", 1, 4), ("T", 1, 3), ("S", 1, 0, 9),
    ("T", 1, 2), ("S", 1, 0, 8), ("S", 1, 0, 7), ("T", 1, 1), ("S", 1, 1, 8), ("S", 1, 1, 6),
    ("T", 1, 0), ("S", 1, 0, 6), ("S", 1, 0, 5), ("S", 1, 1, 3), ("S", 1, 0, 4), ("S", 1, 1, 4),
    ("F", 0), ("A", 0, 0, 0), ("A", 0, 1, 0), ("S", 1, 1, 2), ("D", 0, 0, 0), ("S", 1, 1, 1),
    ("S", 1, 0, 3), ("D", 1, 0, 0), ("A", 0, 0, 4), ("S", 1, 0, 2), ("A", 0, 0, 1),
    ("A", 0, 1, 8), ("D", 0, 0, 8), ("D", 1, 0, 8), ("A", 0, 0, 5), ("A", 0, 0, 8),
    ("A", 0, 1, 2), ("A", 0, 0, 2), ("A", 0, 1, 4), ("D", 0, 0, 2), ("D", 0, 0, 4),
    ("D", 1, 0, 2), ("A", 0, 1, 1), ("A", 0, 0, 12), ("D", 0, 0, 1), ("D", 1, 0, 4),
    ("A", 0, 0, 9), ("A", 0, 1, 10), ("S", 1, 0, 1), ("D", 0, 0, 10), ("D", 1, 0, 1),
    ("D", 1, 0, 10), ("A", 0, 0, 3), ("A", 0, 0, 6), ("A", 0, 0, 13), ("A", 0, 1, 12),
    ("D", 0, 0, 12), ("A", 0, 1, 6), ("A", 0, 1, 9), ("A", 0, 1, 3), ("F", 1), ("A", 0, 1, 5),
    ("A", 0, 0, 7), ("A", 0, 0, 10), ("A", 1, 0, 0), ("A", 0, 1, 14), ("A", 1, 1, 0),
    ("D", 0, 0, 3), ("A", 0, 0, 11), ("D", 1, 0, 3), ("D", 0, 0, 5), ("D", 1, 0, 5),
    ("D", 0, 0, 6), ("A", 0, 1, 11), ("D", 1, 0, 6), ("D", 0, 0, 9), ("D", 1, 0, 9),
    ("A", 0, 0, 14), ("D", 0, 0, 11), ("D", 1, 0, 12), ("A", 1, 0, 1), ("A", 0, 1, 7),
    ("D", 0, 0, 7), ("D", 1, 0, 11), ("D", 0, 0, 14), ("D", 1, 0, 14), ("A", 0, 1, 13),
    ("D", 0, 0, 13), ("D", 0, 1, 0), ("D", 1, 1, 0), ("D", 1, 0, 7), ("D", 1, 0, 13),
    ("A", 1, 0, 8), ("A", 0, 0, 15), ("A", 1, 1, 2), ("D", 0, 1, 8), ("A", 1, 0, 2),
    ("A", 1, 1, 4), ("D", 0, 1, 2), ("A", 1, 0, 4), ("D", 1, 1, 8), ("A", 1, 1, 8),
    ("D", 0, 1, 4), ("A", 1, 0, 9), ("D", 1, 1, 2), ("A", 1, 1, 1), ("A", 0, 1, 15),
    ("A", 1, 0, 3), ("D", 0, 0, 15), ("D", 0, 1, 1), ("D", 1, 1, 4), ("A", 1, 1, 6),
    ("D", 0, 1, 10), ("D", 1, 1, 1), ("D", 1, 0, 15), ("A", 1, 0, 5), ("A", 1, 1, 10),
    ("A", 1, 0, 10), ("D", 0, 1, 12), ("D", 1, 1, 10), ("A", 1, 1, 12), ("D", 0, 1, 6),
    ("A", 1, 0, 12), ("D", 1, 1, 12), ("A", 1, 1, 5), ("D", 0, 1, 3), ("D", 1, 1, 6),
    ("A", 1, 1, 9), ("A", 1, 1, 3), ("D", 1, 1, 3), ("A", 1, 0, 6), ("A", 1, 1, 14),
    ("D", 0, 1, 5), ("D", 0, 1, 9), ("A", 1, 0, 11), ("D", 1, 1, 9), ("A", 1, 1, 7),
    ("A", 1, 0, 7), ("A", 1, 1, 13), ("D", 1, 1, 5), ("A", 1, 0, 13), ("D", 0, 1, 7),
    ("D", 0, 1, 11), ("D", 0, 1, 14), ("D", 1, 1, 14), ("D", 1, 1, 7), ("A", 1, 1, 11),
    ("A", 1, 0, 14), ("D", 1, 1, 11), ("D", 0, 1, 13), ("A", 1, 1, 15), ("A", 1, 0, 15),
    ("D", 1, 1, 13), ("D", 0, 1, 15), ("D", 1, 1, 15),
]


class Plan:
    def __init__(self, n_out, n_in, rows, cols):
        self.n_out, self.n_in, self.rows, self.cols = n_out, n_in, rows, cols
        out_bits = [("outer", k) for k in range(n_out.bit_length() - 1)]
        in_bits = [("inner", k) for k in range(1, n_in.bit_length() - 1)]
        ranked = []
        for k in range(max(len(out_bits), len(in_bits))):
            ranked += out_bits[k : k + 1] + in_bits[k : k + 1]
        self.dims = ranked[::-1]
        self.depth = len(ranked)
        self.blocks = 2**self.depth
        self.groups = len(SUM_ORDERS)
        self.parts = len(SUM_ORDERS[0])
        self.group_cols = cols // self.groups

    def canon(self, order, k):
        return sum(((k >> t) & 1) << order[self.depth - 1 - t] for t in range(self.depth))


def kernel(plan, *refs):
    (act_h, grad_h, mw_h, m1_h, m2_h, nt_h, nm_o, n1_o, n2_o, kept_o, proj_o) = refs[:11]
    (act, grad, nt, mw, m1, m2, nm, n1, n2, grad_t, own, snd0, rcv0, total, weights, acc) = refs[11:27]
    depth, blocks, groups, parts = plan.depth, plan.blocks, plan.groups, plan.parts
    rv_flat = refs[27 : 27 + groups * parts * depth]
    (
        load_sem,
        core_send,
        core_recv,
        rs_send,
        rs_recv,
        ag_send,
        ag_recv,
        cg_send,
        cg_recv,
        local,
        group_local,
    ) = refs[27 + groups * parts * depth :]
    rv = {
        (g, p): rv_flat[(g * parts + p) * depth : (g * parts + p + 1) * depth]
        for g in range(groups)
        for p in range(parts)
    }
    wide = plan.group_cols
    R, C = plan.rows, plan.cols

    outer, inner = lax.axis_index("outer"), lax.axis_index("inner")
    place = {"outer": outer, "inner": inner}

    def bit(axis, k):
        return (place[axis] // 2**k) % 2

    def partner(axis, k):
        other = place[axis] + (1 - 2 * bit(axis, k)) * 2**k
        return (other, inner) if axis == "outer" else (outer, other)

    sibling = partner("inner", 0)
    others = [partner(axis, k) for axis, k in plan.dims]

    barrier = pltpu.get_barrier_semaphore()
    for device in [sibling] + others:
        pl.semaphore_signal(barrier, inc=1, device_id=device, device_id_type=MESH)

    def block_at(flip_core, c):
        o, n = outer, inner
        if flip_core:
            n = n + 1 - 2 * bit("inner", 0)
        for j, (axis, k) in enumerate(plan.dims):
            step = ((c // 2**j) % 2) * (1 - 2 * bit(axis, k)) * 2**k
            if axis == "outer":
                o = o + step
            else:
                n = n + step
        return o, n

    def columns(flip_core, c):
        o, n = block_at(flip_core, c)
        return pl.ds(pl.multiple_of((n * plan.n_out + o) * R, R), R)

    sequence = [step[2] for step in STEPS if step[0] == "T" and step[1] == 0]

    first_load = pltpu.make_async_copy(grad_h, grad, local.at[0])
    first_load.start()
    act_loads = {}
    for c in sequence:
        for side in (1, 0):
            load = pltpu.make_async_copy(
                act_h.at[:, columns(side == 1, c)], act.at[side, c], load_sem.at[side, c]
            )
            load.start()
            act_loads[(side, c)] = load
    loads = [
        pltpu.make_async_copy(s, d, local.at[1 + i])
        for i, (s, d) in enumerate([(mw_h, mw), (m1_h, m1), (m2_h, m2), (nt_h, nt)])
    ]
    for load in loads:
        load.start()

    first_load.wait()
    grad_t[...] = grad[...].astype(F32).T.astype(BF16)
    pl.semaphore_wait(barrier, 1 + depth)

    cores, sums, passed, crossed, stores = {}, {}, {}, {}, []
    done = set()

    def once(key, wait):
        if key not in done:
            done.add(key)
            wait()

    def group_span(g):
        return pl.ds(g * wide, wide)

    def term(side, g, c):
        once(("act", side, c), act_loads[(side, c)].wait)
        return jnp.dot(
            grad_t[group_span(g), :], act[side, c], preferred_element_type=F32
        ).astype(BF16)

    def send_term(g, c):
        at = (c, group_span(g))
        snd0[c, group_span(g), :] = term(1, g, c)
        copy = pltpu.make_async_remote_copy(
            src_ref=snd0.at[at],
            dst_ref=rcv0.at[at],
            send_sem=core_send.at[g, c],
            recv_sem=core_recv.at[g, c],
            device_id=sibling,
            device_id_type=MESH,
        )
        copy.start()
        cores[(g, c)] = copy
        own[c, group_span(g), :] = term(0, g, c)

    count = wide // parts
    tile = min(count, 64)

    def gather_terms(g, p, k, steps, last):
        c = plan.canon(SUM_ORDERS[g][p], k)
        once(("core", g, c), cores[(g, c)].wait_recv)
        for t in range(steps):
            sums[(g, p, k + 2 ** (depth - 1 - t))].wait_recv()
        for at in range(0, count, tile):
            span = pl.ds(g * wide + p * count + at, tile)
            value = own[c, span, :].astype(F32) + rcv0[c, span, :].astype(F32)
            for t in range(steps):
                value += rv[(g, p)][t][k, pl.ds(at, tile), :].astype(F32)
            if last:
                total[span, :] = value
            else:
                own[c, span, :] = value.astype(BF16)

    def send_sum(g, p, k):
        order = SUM_ORDERS[g][p]
        high = k.bit_length() - 1
        step = depth - 1 - high
        gather_terms(g, p, k, step, False)
        copy = pltpu.make_async_remote_copy(
            src_ref=own.at[plan.canon(order, k), pl.ds(g * wide + p * count, count)],
            dst_ref=rv[(g, p)][step].at[k - 2**high],
            send_sem=rs_send.at[g * parts + p, k],
            recv_sem=rs_recv.at[g * parts + p, k],
            device_id=others[order[step]],
            device_id_type=MESH,
        )
        copy.start()
        sums[(g, p, k)] = copy

    def update(g):
        for p in range(parts):
            gather_terms(g, p, 0, depth, True)
        once("state", lambda: [load.wait() for load in loads[:3]])
        span = group_span(g)
        gradient = total[span, :].T
        master, first, second = adamw_update(gradient, mw[:, span], m1[:, span], m2[:, span])
        weights[0, g, 0] = master.astype(BF16)
        nm[:, span] = master
        n1[:, span] = first
        n2[:, span] = second
        for i, (s, d) in enumerate([(nm, nm_o), (n1, n1_o), (n2, n2_o)]):
            store = pltpu.make_async_copy(s.at[:, span], d.at[:, span], group_local.at[g, i])
            store.start()
            stores.append(store)

    def pass_on(g, p, q):
        order = GATHER_ORDERS[g][p]
        c = plan.canon(order, q)
        high = q.bit_length() - 1
        if q > 0:
            passed[(g, p, q)].wait_recv()
        rows = pl.ds(p * (R // parts), R // parts)
        for t in range(high + 1, depth):
            e = order[depth - 1 - t]
            copy = pltpu.make_async_remote_copy(
                src_ref=weights.at[0, g, c, rows],
                dst_ref=weights.at[0, g, c + 2**e, rows],
                send_sem=ag_send.at[g * parts + p, q + 2**t],
                recv_sem=ag_recv.at[g * parts + p, q + 2**t],
                device_id=others[e],
                device_id_type=MESH,
            )
            copy.start()
            passed[(g, p, q + 2**t)] = copy
        copy = pltpu.make_async_remote_copy(
            src_ref=weights.at[0, g, c, rows],
            dst_ref=weights.at[1, g, c, rows],
            send_sem=cg_send.at[g * parts + p, c],
            recv_sem=cg_recv.at[g * parts + p, c],
            device_id=sibling,
            device_id_type=MESH,
        )
        copy.start()
        crossed[(g, p, c)] = copy

    inner_mask = sum(2**j for j, (axis, _) in enumerate(plan.dims) if axis == "inner")

    def project(side, g, c):
        span = group_span(g)
        if side == 1:
            for p in range(parts):
                crossed[(g, p, c)].wait_recv()
        elif c & inner_mask == 0:
            o, _ = block_at(False, c)
            keep = pltpu.make_async_copy(
                weights.at[0, g, c],
                kept_o.at[pl.ds(pl.multiple_of(o * R, R), R), span],
                group_local.at[g, 3 + c],
            )
            keep.start()
            stores.append(keep)
        once("next", loads[3].wait)
        share = jnp.dot(
            nt[:, columns(side == 1, c)], weights[side, g, c], preferred_element_type=F32
        )
        if ("acc", g) in done:
            acc[:, span] += share
        else:
            done.add(("acc", g))
            acc[:, span] = share

    run = {"T": send_term, "S": send_sum, "F": update, "A": pass_on, "D": project}
    for step in STEPS:
        run[step[0]](*step[1:])
    proj_o[...] = acc[...].astype(BF16)

    for group in (cores, sums, passed, crossed):
        for copy in group.values():
            copy.wait_send()
    for copy in stores:
        copy.wait()


def local_kernel(activations, output_grads, master_weights, first_moment, second_moment, next_tokens):
    n_out, n_in = lax.axis_size("outer"), lax.axis_size("inner")
    tokens, width = activations.shape
    next_rows = next_tokens.shape[0]
    R, C = master_weights.shape
    plan = Plan(n_out, n_in, R, C)
    B, L, G, n_parts = plan.blocks, plan.depth, plan.groups, plan.groups * plan.parts
    dma = pltpu.SemaphoreType.DMA
    any_spec = pl.BlockSpec(memory_space=pl.ANY)
    arrived = [
        pltpu.VMEM((2 ** (L - 1 - s), plan.group_cols // plan.parts, R), BF16)
        for _ in range(n_parts)
        for s in range(L)
    ]
    results = pl.pallas_call(
        functools.partial(kernel, plan),
        out_shape=(
            jax.ShapeDtypeStruct((R, C), F32),
            jax.ShapeDtypeStruct((R, C), F32),
            jax.ShapeDtypeStruct((R, C), F32),
            jax.ShapeDtypeStruct((n_out * R, C), BF16),
            jax.ShapeDtypeStruct((next_rows, C), BF16),
        ),
        in_specs=[any_spec] * 6,
        out_specs=(any_spec,) * 4 + (pl.BlockSpec(memory_space=pltpu.VMEM),),
        scratch_shapes=[
            pltpu.VMEM((2, B, tokens, R), BF16),
            pltpu.VMEM((tokens, C), BF16),
            pltpu.VMEM((next_rows, width), BF16),
        ]
        + [pltpu.VMEM((R, C), F32)] * 6
        + [
            pltpu.VMEM((C, tokens), BF16),
            pltpu.VMEM((B, C, R), BF16),
            pltpu.VMEM((B, C, R), BF16),
            pltpu.VMEM((B, C, R), BF16),
            pltpu.VMEM((C, R), F32),
            pltpu.VMEM((2, G, B, R, plan.group_cols), BF16),
            pltpu.VMEM((next_rows, C), F32),
        ]
        + arrived
        + [
            dma((2, B)),
            dma((G, B)),
            dma((G, B)),
            dma((n_parts, B)),
            dma((n_parts, B)),
            dma((n_parts, B)),
            dma((n_parts, B)),
            dma((n_parts, B)),
            dma((n_parts, B)),
            dma((5,)),
            dma((G, 3 + B)),
        ],
        compiler_params=pltpu.CompilerParams(
            collective_id=0, has_side_effects=True, vmem_limit_bytes=58 * 2**20
        ),
        cost_estimate=pl.CostEstimate(
            flops=2 * (tokens + next_rows) * width * C,
            bytes_accessed=2 * (tokens + next_rows) * width + 24 * R * C,
            transcendentals=R * C,
        ),
    )(activations, output_grads, master_weights, first_moment, second_moment, next_tokens)
    return hand_on(results)


def copy_kernel(pieces, *refs):
    count = len(refs) // 3
    sources, targets, held, sems = refs[:count], refs[count : 2 * count], refs[2 * count : -1], refs[-1]
    spans = [
        (i, pl.ds(n * (ref.shape[0] // pieces), ref.shape[0] // pieces))
        for i, ref in enumerate(sources)
        for n in range(pieces)
    ]
    ins = [
        pltpu.make_async_copy(sources[i].at[at], held[i].at[at], sems.at[0, n])
        for n, (i, at) in enumerate(spans)
    ]
    outs = [
        pltpu.make_async_copy(held[i].at[at], targets[i].at[at], sems.at[1, n])
        for n, (i, at) in enumerate(spans)
    ]
    for copy in ins:
        copy.start()
    for copy, onward in zip(ins, outs):
        copy.wait()
        onward.start()
    for copy in outs:
        copy.wait()


def hand_on(arrays, pieces=2):
    any_spec = pl.BlockSpec(memory_space=pl.ANY)
    return pl.pallas_call(
        functools.partial(copy_kernel, pieces),
        out_shape=tuple(jax.ShapeDtypeStruct(a.shape, a.dtype) for a in arrays),
        in_specs=[any_spec] * len(arrays),
        out_specs=(any_spec,) * len(arrays),
        scratch_shapes=[pltpu.VMEM(a.shape, a.dtype) for a in arrays]
        + [pltpu.SemaphoreType.DMA((2, pieces * len(arrays)))],
        compiler_params=pltpu.CompilerParams(vmem_limit_bytes=60 * 2**20),
    )(*arrays)


def fits_kernel(mesh):
    n_out, n_in = mesh.shape["outer"], mesh.shape["inner"]
    return n_out == 8 and n_in == 4


def solution(mesh):
    placed = (
        P(("outer", "inner"), None),
        P(("outer", "inner"), None),
        P(("inner", "outer"), None),
        P(("inner", "outer"), None),
        P(("inner", "outer"), None),
        P(("outer", "inner"), None),
    )
    return jax.shard_map(
        local_kernel if fits_kernel(mesh) else local_plain,
        mesh=mesh,
        in_specs=placed,
        out_specs=(
            P(("inner", "outer"), None),
            P(("inner", "outer"), None),
            P(("inner", "outer"), None),
            P("inner", None),
            P(("outer", "inner"), None),
        ),
        check_vma=False,
    )
```

```python
import functools

import jax
import jax.numpy as jnp
from jax import lax
from jax.experimental import pallas as pl
from jax.experimental.pallas import tpu as pltpu
from jax.sharding import PartitionSpec as P

ADAM_STEP = 10
MESH = pl.DeviceIdType.MESH
BF16 = jnp.bfloat16
F32 = jnp.float32


beta_first = 0.9
beta_second = 0.95
learn_rate = 0.002
decay_rate = 0.1
adam_eps = 1e-08


def adamw_update(gradient, master_weights, first_moment, second_moment):
    new_first = beta_first * first_moment + (1.0 - beta_first) * gradient
    new_second = beta_second * second_moment + (1.0 - beta_second) * gradient * gradient
    first_hat = new_first / (1.0 - beta_first**ADAM_STEP)
    second_hat = new_second / (1.0 - beta_second**ADAM_STEP)
    new_master = master_weights - learn_rate * (
        first_hat / (jnp.sqrt(second_hat) + adam_eps) + decay_rate * master_weights
    )
    return (new_master, new_first, new_second)


def rounded_term(columns, output_grads):
    contrib = jnp.einsum(
        "tr,tc->rc", columns, output_grads, preferred_element_type=jnp.float32
    ).astype(jnp.bfloat16)
    contrib = lax.optimization_barrier(contrib)
    return contrib.astype(jnp.float32)


def regroup_features(activations, outer_count, inner_count):
    tok_rows, width = activations.shape
    shard_rows = width // (outer_count * inner_count)
    split_view = activations.reshape(tok_rows, inner_count, outer_count, shard_rows)
    return split_view.transpose(0, 2, 1, 3).reshape(tok_rows, width)


def local_plain(activations, output_grads, master_weights, first_moment, second_moment, next_tokens):
    outer_count = lax.axis_size("outer")
    inner_count = lax.axis_size("inner")
    regrouped = regroup_features(activations, outer_count, inner_count)
    gradient = lax.psum_scatter(
        rounded_term(regrouped, output_grads), ("outer", "inner"), scatter_dimension=0, tiled=True
    )
    new_master, new_first, new_second = adamw_update(
        gradient, master_weights, first_moment, second_moment
    )
    kept_shard = new_master.astype(jnp.bfloat16)
    kept_weights = lax.all_gather(kept_shard, "outer", axis=0, tiled=True)
    projected = jnp.dot(
        next_tokens,
        lax.all_gather(kept_weights, "inner", axis=0, tiled=True),
        preferred_element_type=jnp.float32,
    )
    return (new_master, new_first, new_second, kept_weights, projected.astype(jnp.bfloat16))


SUM_ORDERS = [
    [(3, 0, 1, 2), (2, 1, 3, 0)],
    [(3, 2, 1, 0), (2, 1, 0, 3)],
]
GATHER_ORDERS = [
    [(2, 3, 0, 1), (3, 2, 1, 0)],
    [(3, 0, 2, 1), (2, 1, 3, 0)],
]
STEPS = [
    ("T", 0, 15), ("T", 0, 11), ("T", 0, 14), ("T", 0, 13), ("T", 0, 7), ("S", 0, 0, 15),
    ("S", 0, 1, 15), ("S", 0, 0, 14), ("T", 0, 9), ("S", 0, 1, 14), ("S", 0, 0, 13),
    ("S", 0, 0, 11), ("S", 0, 1, 13), ("S", 0, 1, 11), ("T", 0, 6), ("T", 0, 10), ("S", 0, 0, 12),
    ("S", 0, 0, 7), ("S", 0, 1, 7), ("T", 0, 12), ("T", 0, 5), ("S", 0, 1, 12), ("S", 0, 0, 10),
    ("T", 0, 8), ("T", 0, 4), ("S", 0, 1, 10), ("S", 0, 0, 9), ("S", 0, 1, 9), ("T", 0, 3),
    ("S", 0, 1, 6), ("S", 0, 0, 8), ("S", 0, 0, 5), ("S", 0, 1, 8), ("T", 0, 2), ("S", 0, 1, 3),
    ("T", 0, 1), ("S", 0, 0, 6), ("S", 0, 1, 5), ("S", 0, 0, 3), ("T", 0, 0), ("T", 1, 15),
    ("T", 1, 14), ("S", 0, 0, 4), ("T", 1, 7), ("S", 0, 1, 4), ("T", 1, 13), ("S", 0, 1, 2),
    ("S", 1, 0, 15), ("S", 1, 1, 15), ("S", 1, 0, 14), ("S", 1, 1, 13), ("S", 1, 1, 14),
    ("T", 1, 12), ("S", 1, 0, 13), ("S", 1, 1, 11), ("T", 1, 6), ("T", 1, 11), ("T", 1, 10),
    ("S", 1, 0, 12), ("S", 1, 1, 9), ("T", 1, 5), ("S", 0, 1, 1), ("S", 1, 1, 12), ("S", 0, 0, 2),
    ("S", 1, 0, 11), ("S", 1, 0, 10), ("S", 1, 1, 7), ("T", 1, 9), ("S", 0, 0, 1),
    ("S", 1, 1, 10), ("T", 1, 8), ("S", 1, 1, 5), ("T", 1, 4), ("T", 1, 3), ("S", 1, 0, 9),
    ("T", 1, 2), ("S", 1, 0, 8), ("S", 1, 0, 7), ("T", 1, 1), ("S", 1, 1, 8), ("S", 1, 1, 6),
    ("T", 1, 0), ("S", 1, 0, 6), ("S", 1, 0, 5), ("S", 1, 1, 3), ("S", 1, 0, 4), ("S", 1, 1, 4),
    ("F", 0), ("A", 0, 0, 0), ("A", 0, 1, 0), ("S", 1, 1, 2), ("D", 0, 0, 0), ("S", 1, 1, 1),
    ("S", 1, 0, 3), ("D", 1, 0, 0), ("A", 0, 0, 4), ("S", 1, 0, 2), ("A", 0, 0, 1),
    ("A", 0, 1, 8), ("D", 0, 0, 8), ("D", 1, 0, 8), ("A", 0, 0, 5), ("A", 0, 0, 8),
    ("A", 0, 1, 2), ("A", 0, 0, 2), ("A", 0, 1, 4), ("D", 0, 0, 2), ("D", 0, 0, 4),
    ("D", 1, 0, 2), ("A", 0, 1, 1), ("A", 0, 0, 12), ("D", 0, 0, 1), ("D", 1, 0, 4),
    ("A", 0, 0, 9), ("A", 0, 1, 10), ("S", 1, 0, 1), ("D", 0, 0, 10), ("D", 1, 0, 1),
    ("D", 1, 0, 10), ("A", 0, 0, 3), ("A", 0, 0, 6), ("A", 0, 0, 13), ("A", 0, 1, 12),
    ("D", 0, 0, 12), ("A", 0, 1, 6), ("A", 0, 1, 9), ("A", 0, 1, 3), ("F", 1), ("A", 0, 1, 5),
    ("A", 0, 0, 7), ("A", 0, 0, 10), ("A", 1, 0, 0), ("A", 0, 1, 14), ("A", 1, 1, 0),
    ("D", 0, 0, 3), ("A", 0, 0, 11), ("D", 1, 0, 3), ("D", 0, 0, 5), ("D", 1, 0, 5),
    ("D", 0, 0, 6), ("A", 0, 1, 11), ("D", 1, 0, 6), ("D", 0, 0, 9), ("D", 1, 0, 9),
    ("A", 0, 0, 14), ("D", 0, 0, 11), ("D", 1, 0, 12), ("A", 1, 0, 1), ("A", 0, 1, 7),
    ("D", 0, 0, 7), ("D", 1, 0, 11), ("D", 0, 0, 14), ("D", 1, 0, 14), ("A", 0, 1, 13),
    ("D", 0, 0, 13), ("D", 0, 1, 0), ("D", 1, 1, 0), ("D", 1, 0, 7), ("D", 1, 0, 13),
    ("A", 1, 0, 8), ("A", 0, 0, 15), ("A", 1, 1, 2), ("D", 0, 1, 8), ("A", 1, 0, 2),
    ("A", 1, 1, 4), ("D", 0, 1, 2), ("A", 1, 0, 4), ("D", 1, 1, 8), ("A", 1, 1, 8),
    ("D", 0, 1, 4), ("A", 1, 0, 9), ("D", 1, 1, 2), ("A", 1, 1, 1), ("A", 0, 1, 15),
    ("A", 1, 0, 3), ("D", 0, 0, 15), ("D", 0, 1, 1), ("D", 1, 1, 4), ("A", 1, 1, 6),
    ("D", 0, 1, 10), ("D", 1, 1, 1), ("D", 1, 0, 15), ("A", 1, 0, 5), ("A", 1, 1, 10),
    ("A", 1, 0, 10), ("D", 0, 1, 12), ("D", 1, 1, 10), ("A", 1, 1, 12), ("D", 0, 1, 6),
    ("A", 1, 0, 12), ("D", 1, 1, 12), ("A", 1, 1, 5), ("D", 0, 1, 3), ("D", 1, 1, 6),
    ("A", 1, 1, 9), ("A", 1, 1, 3), ("D", 1, 1, 3), ("A", 1, 0, 6), ("A", 1, 1, 14),
    ("D", 0, 1, 5), ("D", 0, 1, 9), ("A", 1, 0, 11), ("D", 1, 1, 9), ("A", 1, 1, 7),
    ("A", 1, 0, 7), ("A", 1, 1, 13), ("D", 1, 1, 5), ("A", 1, 0, 13), ("D", 0, 1, 7),
    ("D", 0, 1, 11), ("D", 0, 1, 14), ("D", 1, 1, 14), ("D", 1, 1, 7), ("A", 1, 1, 11),
    ("A", 1, 0, 14), ("D", 1, 1, 11), ("D", 0, 1, 13), ("A", 1, 1, 15), ("A", 1, 0, 15),
    ("D", 1, 1, 13), ("D", 0, 1, 15), ("D", 1, 1, 15),
]


class Plan:
    def __init__(self, n_out, n_in, rows, cols):
        self.n_out, self.n_in, self.rows, self.cols = n_out, n_in, rows, cols
        out_bits = [("outer", k) for k in range(n_out.bit_length() - 1)]
        in_bits = [("inner", k) for k in range(1, n_in.bit_length() - 1)]
        ranked = []
        for k in range(max(len(out_bits), len(in_bits))):
            ranked += out_bits[k : k + 1] + in_bits[k : k + 1]
        self.dims = ranked[::-1]
        self.depth = len(ranked)
        self.blocks = 2**self.depth
        self.groups = len(SUM_ORDERS)
        self.parts = len(SUM_ORDERS[0])
        self.group_cols = cols // self.groups

    def canon(self, order, k):
        return sum(((k >> t) & 1) << order[self.depth - 1 - t] for t in range(self.depth))


def kernel(plan, *refs):
    (act_h, grad_h, mw_h, m1_h, m2_h, nt_h, nm_o, n1_o, n2_o, kept_o, proj_o) = refs[:11]
    (act, grad, nt, mw, m1, m2, nm, n1, n2, grad_t, own, snd0, rcv0, total, weights, acc) = refs[11:27]
    depth, blocks, groups, parts = plan.depth, plan.blocks, plan.groups, plan.parts
    rv_flat = refs[27 : 27 + groups * parts * depth]
    (
        load_sem,
        core_send,
        core_recv,
        rs_send,
        rs_recv,
        ag_send,
        ag_recv,
        cg_send,
        cg_recv,
        local,
        group_local,
    ) = refs[27 + groups * parts * depth :]
    rv = {
        (g, p): rv_flat[(g * parts + p) * depth : (g * parts + p + 1) * depth]
        for g in range(groups)
        for p in range(parts)
    }
    wide = plan.group_cols
    R, C = plan.rows, plan.cols

    outer, inner = lax.axis_index("outer"), lax.axis_index("inner")
    place = {"outer": outer, "inner": inner}

    def bit(axis, k):
        return (place[axis] // 2**k) % 2

    def partner(axis, k):
        other = place[axis] + (1 - 2 * bit(axis, k)) * 2**k
        return (other, inner) if axis == "outer" else (outer, other)

    sibling = partner("inner", 0)
    others = [partner(axis, k) for axis, k in plan.dims]

    barrier = pltpu.get_barrier_semaphore()
    for device in [sibling] + others:
        pl.semaphore_signal(barrier, inc=1, device_id=device, device_id_type=MESH)

    def block_at(flip_core, c):
        o, n = outer, inner
        if flip_core:
            n = n + 1 - 2 * bit("inner", 0)
        for j, (axis, k) in enumerate(plan.dims):
            step = ((c // 2**j) % 2) * (1 - 2 * bit(axis, k)) * 2**k
            if axis == "outer":
                o = o + step
            else:
                n = n + step
        return o, n

    def columns(flip_core, c):
        o, n = block_at(flip_core, c)
        return pl.ds(pl.multiple_of((n * plan.n_out + o) * R, R), R)

    sequence = [step[2] for step in STEPS if step[0] == "T" and step[1] == 0]

    first_load = pltpu.make_async_copy(grad_h, grad, local.at[0])
    first_load.start()
    act_loads = {}
    for c in sequence:
        for side in (1, 0):
            load = pltpu.make_async_copy(
                act_h.at[:, columns(side == 1, c)], act.at[side, c], load_sem.at[side, c]
            )
            load.start()
            act_loads[(side, c)] = load
    loads = [
        pltpu.make_async_copy(s, d, local.at[1 + i])
        for i, (s, d) in enumerate([(mw_h, mw), (m1_h, m1), (m2_h, m2), (nt_h, nt)])
    ]
    for load in loads:
        load.start()

    first_load.wait()
    grad_t[...] = grad[...].astype(F32).T.astype(BF16)
    pl.semaphore_wait(barrier, 1 + depth)

    cores, sums, passed, crossed, met, stores = {}, {}, {}, {}, {}, []
    done = set()

    def once(key, wait):
        if key not in done:
            done.add(key)
            wait()

    def group_span(g):
        return pl.ds(g * wide, wide)

    def term(side, g, c):
        once(("act", side, c), act_loads[(side, c)].wait)
        return jnp.dot(
            grad_t[group_span(g), :], act[side, c], preferred_element_type=F32
        ).astype(BF16)

    def send_term(g, c):
        at = (c, group_span(g))
        snd0[c, group_span(g), :] = term(1, g, c)
        copy = pltpu.make_async_remote_copy(
            src_ref=snd0.at[at],
            dst_ref=rcv0.at[at],
            send_sem=core_send.at[0],
            recv_sem=core_recv.at[g, c],
            device_id=sibling,
            device_id_type=MESH,
        )
        copy.start()
        cores[(g, c)] = copy
        own[c, group_span(g), :] = term(0, g, c)

    count = wide // parts
    tile = min(count, 64)

    def gather_terms(g, p, k, steps, last):
        c = plan.canon(SUM_ORDERS[g][p], k)
        once(("core", g, c), cores[(g, c)].wait_recv)
        for t in range(steps):
            sums[(g, p, k + 2 ** (depth - 1 - t))].wait_recv()
        for at in range(0, count, tile):
            span = pl.ds(g * wide + p * count + at, tile)
            value = own[c, span, :].astype(F32) + rcv0[c, span, :].astype(F32)
            for t in range(steps):
                value += rv[(g, p)][t][k, pl.ds(at, tile), :].astype(F32)
            if last:
                total[span, :] = value
            else:
                own[c, span, :] = value.astype(BF16)

    def send_sum(g, p, k):
        order = SUM_ORDERS[g][p]
        high = k.bit_length() - 1
        step = depth - 1 - high
        gather_terms(g, p, k, step, False)
        copy = pltpu.make_async_remote_copy(
            src_ref=own.at[plan.canon(order, k), pl.ds(g * wide + p * count, count)],
            dst_ref=rv[(g, p)][step].at[k - 2**high],
            send_sem=rs_send.at[0],
            recv_sem=rs_recv.at[g * parts + p, k],
            device_id=others[order[step]],
            device_id_type=MESH,
        )
        copy.start()
        sums[(g, p, k)] = copy

    def update(g):
        for p in range(parts):
            gather_terms(g, p, 0, depth, True)
        once("state", lambda: [load.wait() for load in loads[:3]])
        span = group_span(g)
        gradient = total[span, :].T
        master, first, second = adamw_update(gradient, mw[:, span], m1[:, span], m2[:, span])
        weights[0, g, 0] = master.astype(BF16)
        nm[:, span] = master
        n1[:, span] = first
        n2[:, span] = second
        for i, (s, d) in enumerate([(nm, nm_o), (n1, n1_o), (n2, n2_o)]):
            store = pltpu.make_async_copy(s.at[:, span], d.at[:, span], group_local.at[g, i])
            store.start()
            stores.append(store)

    def pass_on(g, p, q):
        order = GATHER_ORDERS[g][p]
        c = plan.canon(order, q)
        high = q.bit_length() - 1
        if q > 0:
            passed[(g, p, q)].wait_recv()
        rows = pl.ds(p * (R // parts), R // parts)
        for t in range(high + 1, depth):
            e = order[depth - 1 - t]
            copy = pltpu.make_async_remote_copy(
                src_ref=weights.at[0, g, c, rows],
                dst_ref=weights.at[0, g, c + 2**e, rows],
                send_sem=ag_send.at[0],
                recv_sem=ag_recv.at[g * parts + p, q + 2**t],
                device_id=others[e],
                device_id_type=MESH,
            )
            copy.start()
            passed[(g, p, q + 2**t)] = copy
        met[(g, c)] = met.get((g, c), 0) + 1
        if met[(g, c)] == parts:
            copy = pltpu.make_async_remote_copy(
                src_ref=weights.at[0, g, c],
                dst_ref=weights.at[1, g, c],
                send_sem=cg_send.at[0],
                recv_sem=cg_recv.at[g, c],
                device_id=sibling,
                device_id_type=MESH,
            )
            copy.start()
            crossed[(g, c)] = copy

    inner_mask = sum(2**j for j, (axis, _) in enumerate(plan.dims) if axis == "inner")

    def project(side, g, c):
        span = group_span(g)
        if side == 1:
            crossed[(g, c)].wait_recv()
        elif c & inner_mask == 0:
            o, _ = block_at(False, c)
            keep = pltpu.make_async_copy(
                weights.at[0, g, c],
                kept_o.at[pl.ds(pl.multiple_of(o * R, R), R), span],
                group_local.at[g, 3 + c],
            )
            keep.start()
            stores.append(keep)
        once("next", loads[3].wait)
        share = jnp.dot(
            nt[:, columns(side == 1, c)], weights[side, g, c], preferred_element_type=F32
        )
        if ("acc", g) in done:
            acc[:, span] += share
        else:
            done.add(("acc", g))
            acc[:, span] = share

    run = {"T": send_term, "S": send_sum, "F": update, "A": pass_on, "D": project}
    for step in STEPS:
        run[step[0]](*step[1:])
    proj_o[...] = acc[...].astype(BF16)

    sent = [
        (core_send, rcv0),
        (rs_send, own.at[pl.ds(1, blocks - 1)]),
        (ag_send, weights.at[0, :, pl.ds(1, blocks - 1)]),
        (cg_send, weights.at[0]),
    ]
    for sem, ref in sent:
        pltpu.make_async_copy(ref, ref, sem.at[0]).wait()
    for copy in stores:
        copy.wait()


def local_kernel(activations, output_grads, master_weights, first_moment, second_moment, next_tokens):
    n_out, n_in = lax.axis_size("outer"), lax.axis_size("inner")
    tokens, width = activations.shape
    next_rows = next_tokens.shape[0]
    R, C = master_weights.shape
    plan = Plan(n_out, n_in, R, C)
    B, L, G, n_parts = plan.blocks, plan.depth, plan.groups, plan.groups * plan.parts
    dma = pltpu.SemaphoreType.DMA
    any_spec = pl.BlockSpec(memory_space=pl.ANY)
    arrived = [
        pltpu.VMEM((2 ** (L - 1 - s), plan.group_cols // plan.parts, R), BF16)
        for _ in range(n_parts)
        for s in range(L)
    ]
    results = pl.pallas_call(
        functools.partial(kernel, plan),
        out_shape=(
            jax.ShapeDtypeStruct((R, C), F32),
            jax.ShapeDtypeStruct((R, C), F32),
            jax.ShapeDtypeStruct((R, C), F32),
            jax.ShapeDtypeStruct((n_out * R, C), BF16),
            jax.ShapeDtypeStruct((next_rows, C), BF16),
        ),
        in_specs=[any_spec] * 6,
        out_specs=(any_spec,) * 4 + (pl.BlockSpec(memory_space=pltpu.VMEM),),
        scratch_shapes=[
            pltpu.VMEM((2, B, tokens, R), BF16),
            pltpu.VMEM((tokens, C), BF16),
            pltpu.VMEM((next_rows, width), BF16),
        ]
        + [pltpu.VMEM((R, C), F32)] * 6
        + [
            pltpu.VMEM((C, tokens), BF16),
            pltpu.VMEM((B, C, R), BF16),
            pltpu.VMEM((B, C, R), BF16),
            pltpu.VMEM((B, C, R), BF16),
            pltpu.VMEM((C, R), F32),
            pltpu.VMEM((2, G, B, R, plan.group_cols), BF16),
            pltpu.VMEM((next_rows, C), F32),
        ]
        + arrived
        + [
            dma((2, B)),
            dma((1,)),
            dma((G, B)),
            dma((1,)),
            dma((n_parts, B)),
            dma((1,)),
            dma((n_parts, B)),
            dma((1,)),
            dma((G, B)),
            dma((5,)),
            dma((G, 3 + B)),
        ],
        compiler_params=pltpu.CompilerParams(
            collective_id=0, has_side_effects=True, vmem_limit_bytes=58 * 2**20
        ),
        cost_estimate=pl.CostEstimate(
            flops=2 * (tokens + next_rows) * width * C,
            bytes_accessed=2 * (tokens + next_rows) * width + 24 * R * C,
            transcendentals=R * C,
        ),
    )(activations, output_grads, master_weights, first_moment, second_moment, next_tokens)
    return hand_on(results)


def copy_kernel(pieces, *refs):
    count = len(refs) // 3
    sources, targets, held, sems = refs[:count], refs[count : 2 * count], refs[2 * count : -1], refs[-1]
    spans = [
        (i, pl.ds(n * (ref.shape[0] // pieces), ref.shape[0] // pieces))
        for i, ref in enumerate(sources)
        for n in range(pieces)
    ]
    ins = [
        pltpu.make_async_copy(sources[i].at[at], held[i].at[at], sems.at[0, n])
        for n, (i, at) in enumerate(spans)
    ]
    outs = [
        pltpu.make_async_copy(held[i].at[at], targets[i].at[at], sems.at[1, n])
        for n, (i, at) in enumerate(spans)
    ]
    for copy in ins:
        copy.start()
    for copy, onward in zip(ins, outs):
        copy.wait()
        onward.start()
    for copy in outs:
        copy.wait()


def hand_on(arrays, pieces=4):
    any_spec = pl.BlockSpec(memory_space=pl.ANY)
    return pl.pallas_call(
        functools.partial(copy_kernel, pieces),
        out_shape=tuple(jax.ShapeDtypeStruct(a.shape, a.dtype) for a in arrays),
        in_specs=[any_spec] * len(arrays),
        out_specs=(any_spec,) * len(arrays),
        scratch_shapes=[pltpu.VMEM(a.shape, a.dtype) for a in arrays]
        + [pltpu.SemaphoreType.DMA((2, pieces * len(arrays)))],
        compiler_params=pltpu.CompilerParams(vmem_limit_bytes=60 * 2**20),
    )(*arrays)


def fits_kernel(mesh):
    n_out, n_in = mesh.shape["outer"], mesh.shape["inner"]
    return n_out == 8 and n_in == 4


def solution(mesh):
    placed = (
        P(("outer", "inner"), None),
        P(("outer", "inner"), None),
        P(("inner", "outer"), None),
        P(("inner", "outer"), None),
        P(("inner", "outer"), None),
        P(("outer", "inner"), None),
    )
    return jax.shard_map(
        local_kernel if fits_kernel(mesh) else local_plain,
        mesh=mesh,
        in_specs=placed,
        out_specs=(
            P(("inner", "outer"), None),
            P(("inner", "outer"), None),
            P(("inner", "outer"), None),
            P("inner", None),
            P(("outer", "inner"), None),
        ),
        check_vma=False,
    )
```

```python
import functools

import jax
import jax.numpy as jnp
from jax import lax
from jax.experimental import pallas as pl
from jax.experimental.pallas import tpu as pltpu
from jax.sharding import PartitionSpec as P

ADAM_STEP = 10
MESH = pl.DeviceIdType.MESH
BF16 = jnp.bfloat16
F32 = jnp.float32


beta_first = 0.9
beta_second = 0.95
learn_rate = 0.002
decay_rate = 0.1
adam_eps = 1e-08


def adamw_update(gradient, master_weights, first_moment, second_moment):
    new_first = beta_first * first_moment + (1.0 - beta_first) * gradient
    new_second = beta_second * second_moment + (1.0 - beta_second) * gradient * gradient
    first_hat = new_first / (1.0 - beta_first**ADAM_STEP)
    second_hat = new_second / (1.0 - beta_second**ADAM_STEP)
    new_master = master_weights - learn_rate * (
        first_hat / (jnp.sqrt(second_hat) + adam_eps) + decay_rate * master_weights
    )
    return (new_master, new_first, new_second)


def rounded_term(columns, output_grads):
    contrib = jnp.einsum(
        "tr,tc->rc", columns, output_grads, preferred_element_type=jnp.float32
    ).astype(jnp.bfloat16)
    contrib = lax.optimization_barrier(contrib)
    return contrib.astype(jnp.float32)


def regroup_features(activations, outer_count, inner_count):
    tok_rows, width = activations.shape
    shard_rows = width // (outer_count * inner_count)
    split_view = activations.reshape(tok_rows, inner_count, outer_count, shard_rows)
    return split_view.transpose(0, 2, 1, 3).reshape(tok_rows, width)


def local_plain(activations, output_grads, master_weights, first_moment, second_moment, next_tokens):
    outer_count = lax.axis_size("outer")
    inner_count = lax.axis_size("inner")
    regrouped = regroup_features(activations, outer_count, inner_count)
    gradient = lax.psum_scatter(
        rounded_term(regrouped, output_grads), ("outer", "inner"), scatter_dimension=0, tiled=True
    )
    new_master, new_first, new_second = adamw_update(
        gradient, master_weights, first_moment, second_moment
    )
    kept_shard = new_master.astype(jnp.bfloat16)
    kept_weights = lax.all_gather(kept_shard, "outer", axis=0, tiled=True)
    projected = jnp.dot(
        next_tokens,
        lax.all_gather(kept_weights, "inner", axis=0, tiled=True),
        preferred_element_type=jnp.float32,
    )
    return (new_master, new_first, new_second, kept_weights, projected.astype(jnp.bfloat16))


SUM_ORDERS = [
    [(3, 0, 2, 1), (2, 1, 3, 0)],
    [(3, 2, 1, 0), (2, 3, 0, 1)],
]
GATHER_ORDERS = [
    [(2, 3, 0, 1), (3, 2, 1, 0)],
    [(3, 1, 2, 0), (2, 1, 3, 0)],
]
STEPS = [
    ("T", 0, 15), ("T", 0, 13), ("T", 0, 14), ("T", 0, 11), ("T", 0, 7), ("S", 0, 0, 15),
    ("S", 0, 1, 15), ("S", 0, 0, 14), ("S", 0, 1, 14), ("S", 0, 0, 11), ("S", 0, 0, 13),
    ("S", 0, 1, 11), ("S", 0, 1, 13), ("T", 0, 9), ("T", 0, 6), ("S", 0, 0, 7), ("S", 0, 1, 7),
    ("T", 0, 12), ("T", 0, 10), ("S", 0, 0, 12), ("S", 0, 1, 12), ("T", 0, 5), ("T", 0, 8),
    ("S", 0, 0, 10), ("S", 0, 1, 10), ("S", 0, 0, 9), ("S", 0, 1, 6), ("T", 0, 4), ("S", 0, 1, 9),
    ("S", 0, 0, 8), ("S", 0, 0, 6), ("S", 0, 0, 3), ("S", 0, 1, 3), ("T", 0, 3), ("S", 0, 1, 8),
    ("T", 0, 2), ("T", 0, 1), ("S", 0, 1, 2), ("T", 0, 0), ("S", 0, 0, 5), ("S", 0, 1, 5),
    ("S", 0, 1, 4), ("T", 1, 15), ("S", 0, 0, 4), ("S", 0, 0, 2), ("T", 1, 14), ("T", 1, 13),
    ("T", 1, 12), ("S", 1, 0, 15), ("S", 1, 1, 15), ("T", 1, 11), ("S", 1, 0, 14),
    ("S", 1, 1, 14), ("S", 1, 0, 13), ("S", 1, 1, 13), ("S", 0, 0, 1), ("S", 1, 0, 12),
    ("S", 0, 1, 1), ("S", 1, 1, 12), ("S", 1, 0, 11), ("S", 1, 1, 7), ("T", 1, 7), ("T", 1, 10),
    ("T", 1, 5), ("T", 1, 9), ("T", 1, 6), ("S", 1, 1, 11), ("S", 1, 0, 10), ("S", 1, 0, 7),
    ("S", 1, 1, 10), ("S", 1, 0, 5), ("S", 1, 0, 9), ("F", 0), ("A", 0, 0, 0), ("A", 0, 1, 0),
    ("S", 1, 1, 9), ("S", 1, 0, 6), ("S", 1, 1, 6), ("S", 1, 1, 5), ("T", 1, 8), ("T", 1, 4),
    ("A", 0, 0, 1), ("T", 1, 3), ("T", 1, 2), ("A", 0, 0, 4), ("S", 1, 0, 8), ("S", 1, 1, 8),
    ("S", 1, 0, 4), ("S", 1, 1, 4), ("S", 1, 0, 3), ("A", 0, 1, 8), ("S", 1, 1, 3),
    ("A", 0, 0, 8), ("T", 1, 1), ("A", 0, 1, 2), ("A", 0, 0, 2), ("A", 0, 1, 4), ("T", 1, 0),
    ("D", 0, 0, 0), ("A", 0, 1, 1), ("S", 1, 0, 2), ("S", 1, 1, 2), ("D", 1, 0, 0),
    ("D", 0, 0, 1), ("S", 1, 0, 1), ("D", 0, 0, 2), ("A", 0, 0, 3), ("A", 0, 0, 5),
    ("D", 1, 0, 1), ("D", 1, 0, 2), ("A", 0, 0, 9), ("D", 0, 0, 4), ("A", 0, 1, 3),
    ("D", 0, 0, 3), ("S", 1, 1, 1), ("D", 1, 0, 4), ("A", 0, 0, 12), ("D", 0, 0, 8),
    ("D", 1, 0, 8), ("D", 1, 0, 3), ("A", 0, 1, 10), ("D", 0, 0, 10), ("A", 0, 0, 6),
    ("A", 0, 1, 6), ("D", 0, 0, 6), ("D", 1, 0, 10), ("A", 0, 1, 12), ("D", 0, 0, 12), ("F", 1),
    ("A", 0, 1, 5), ("A", 0, 0, 7), ("A", 0, 1, 9), ("A", 0, 0, 10), ("A", 0, 0, 11),
    ("A", 0, 1, 11), ("A", 0, 0, 13), ("A", 0, 1, 14), ("A", 1, 0, 0), ("A", 1, 1, 0),
    ("A", 0, 1, 7), ("D", 0, 0, 5), ("A", 0, 1, 13), ("A", 0, 0, 14), ("D", 1, 0, 5),
    ("D", 1, 0, 6), ("D", 0, 0, 7), ("D", 0, 0, 9), ("A", 0, 0, 15), ("D", 1, 0, 7),
    ("A", 1, 0, 8), ("D", 1, 0, 9), ("D", 0, 0, 11), ("D", 1, 0, 11), ("D", 1, 0, 12),
    ("D", 0, 0, 13), ("D", 1, 0, 13), ("A", 1, 0, 2), ("A", 1, 1, 2), ("A", 1, 1, 8),
    ("D", 0, 0, 14), ("A", 0, 1, 15), ("A", 1, 0, 1), ("A", 1, 0, 4), ("D", 1, 0, 14),
    ("D", 0, 0, 15), ("D", 0, 1, 0), ("A", 1, 1, 1), ("A", 1, 1, 4), ("A", 1, 0, 10),
    ("A", 1, 1, 10), ("D", 1, 0, 15), ("A", 1, 0, 6), ("D", 1, 1, 0), ("A", 1, 0, 9),
    ("D", 0, 1, 1), ("A", 1, 0, 3), ("D", 1, 1, 1), ("D", 0, 1, 2), ("D", 1, 1, 2),
    ("A", 1, 0, 12), ("A", 1, 1, 6), ("A", 1, 1, 9), ("D", 0, 1, 4), ("D", 1, 1, 4),
    ("D", 0, 1, 5), ("D", 0, 1, 8), ("A", 1, 0, 5), ("A", 1, 1, 12), ("A", 1, 1, 3),
    ("A", 1, 1, 5), ("A", 1, 0, 14), ("D", 0, 1, 3), ("D", 1, 1, 5), ("A", 1, 1, 14),
    ("D", 0, 1, 6), ("A", 1, 0, 7), ("D", 1, 1, 6), ("A", 1, 0, 11), ("D", 1, 1, 3),
    ("D", 1, 1, 8), ("D", 0, 1, 9), ("A", 1, 1, 7), ("A", 1, 1, 11), ("A", 1, 0, 13),
    ("D", 1, 1, 9), ("D", 0, 1, 10), ("D", 1, 1, 10), ("D", 0, 1, 11), ("A", 1, 1, 13),
    ("D", 0, 1, 7), ("A", 1, 0, 15), ("D", 1, 1, 11), ("D", 0, 1, 12), ("D", 1, 1, 12),
    ("D", 0, 1, 13), ("A", 1, 1, 15), ("D", 1, 1, 7), ("D", 1, 1, 13), ("D", 0, 1, 14),
    ("D", 1, 1, 14), ("D", 0, 1, 15), ("D", 1, 1, 15),
]


class Plan:
    def __init__(self, n_out, n_in, rows, cols):
        self.n_out, self.n_in, self.rows, self.cols = n_out, n_in, rows, cols
        out_bits = [("outer", k) for k in range(n_out.bit_length() - 1)]
        in_bits = [("inner", k) for k in range(1, n_in.bit_length() - 1)]
        ranked = []
        for k in range(max(len(out_bits), len(in_bits))):
            ranked += out_bits[k : k + 1] + in_bits[k : k + 1]
        self.dims = ranked[::-1]
        self.depth = len(ranked)
        self.blocks = 2**self.depth
        self.groups = len(SUM_ORDERS)
        self.parts = len(SUM_ORDERS[0])
        self.group_cols = cols // self.groups

    def canon(self, order, k):
        return sum(((k >> t) & 1) << order[self.depth - 1 - t] for t in range(self.depth))


def kernel(plan, *refs):
    (act_h, grad_h, mw_h, m1_h, m2_h, nt_h, nm_o, n1_o, n2_o, kept_o, proj_o) = refs[:11]
    (act, grad, nt, mw, m1, m2, nm, n1, n2, grad_t, own, snd0, rcv0, total, weights, acc) = refs[11:27]
    depth, blocks, groups, parts = plan.depth, plan.blocks, plan.groups, plan.parts
    rv_flat = refs[27 : 27 + groups * parts * depth]
    (
        load_sem,
        core_send,
        core_recv,
        rs_send,
        rs_recv,
        ag_send,
        ag_recv,
        cg_send,
        cg_recv,
        local,
        group_local,
    ) = refs[27 + groups * parts * depth :]
    rv = {
        (g, p): rv_flat[(g * parts + p) * depth : (g * parts + p + 1) * depth]
        for g in range(groups)
        for p in range(parts)
    }
    wide = plan.group_cols
    R, C = plan.rows, plan.cols

    outer, inner = lax.axis_index("outer"), lax.axis_index("inner")
    place = {"outer": outer, "inner": inner}

    def bit(axis, k):
        return (place[axis] // 2**k) % 2

    def partner(axis, k):
        other = place[axis] + (1 - 2 * bit(axis, k)) * 2**k
        return (other, inner) if axis == "outer" else (outer, other)

    sibling = partner("inner", 0)
    others = [partner(axis, k) for axis, k in plan.dims]

    barrier = pltpu.get_barrier_semaphore()
    for device in [sibling] + others:
        pl.semaphore_signal(barrier, inc=1, device_id=device, device_id_type=MESH)

    def block_at(flip_core, c):
        o, n = outer, inner
        if flip_core:
            n = n + 1 - 2 * bit("inner", 0)
        for j, (axis, k) in enumerate(plan.dims):
            step = ((c // 2**j) % 2) * (1 - 2 * bit(axis, k)) * 2**k
            if axis == "outer":
                o = o + step
            else:
                n = n + step
        return o, n

    def columns(flip_core, c):
        o, n = block_at(flip_core, c)
        return pl.ds(pl.multiple_of((n * plan.n_out + o) * R, R), R)

    sequence = [step[2] for step in STEPS if step[0] == "T" and step[1] == 0]

    first_load = pltpu.make_async_copy(grad_h, grad, local.at[0])
    first_load.start()
    act_loads = {}
    for c in sequence:
        for side in (1, 0):
            load = pltpu.make_async_copy(
                act_h.at[:, columns(side == 1, c)], act.at[side, c], load_sem.at[side, c]
            )
            load.start()
            act_loads[(side, c)] = load
    loads = [
        pltpu.make_async_copy(s, d, local.at[1 + i])
        for i, (s, d) in enumerate([(mw_h, mw), (m1_h, m1), (m2_h, m2), (nt_h, nt)])
    ]
    for load in loads:
        load.start()

    first_load.wait()
    grad_t[...] = grad[...].astype(F32).T.astype(BF16)
    pl.semaphore_wait(barrier, 1 + depth)

    cores, sums, passed, crossed, met, stores = {}, {}, {}, {}, {}, []
    done = set()

    def once(key, wait):
        if key not in done:
            done.add(key)
            wait()

    def group_span(g):
        return pl.ds(g * wide, wide)

    def term(side, g, c):
        once(("act", side, c), act_loads[(side, c)].wait)
        return jnp.dot(
            grad_t[group_span(g), :], act[side, c], preferred_element_type=F32
        ).astype(BF16)

    def send_term(g, c):
        at = (c, group_span(g))
        snd0[c, group_span(g), :] = term(1, g, c)
        copy = pltpu.make_async_remote_copy(
            src_ref=snd0.at[at],
            dst_ref=rcv0.at[at],
            send_sem=core_send.at[0],
            recv_sem=core_recv.at[g, c],
            device_id=sibling,
            device_id_type=MESH,
        )
        copy.start()
        cores[(g, c)] = copy
        own[c, group_span(g), :] = term(0, g, c)

    count = wide // parts
    tile = min(count, 64)

    def gather_terms(g, p, k, steps, last):
        c = plan.canon(SUM_ORDERS[g][p], k)
        once(("core", g, c), cores[(g, c)].wait_recv)
        for t in range(steps):
            sums[(g, p, k + 2 ** (depth - 1 - t))].wait_recv()
        for at in range(0, count, tile):
            span = pl.ds(g * wide + p * count + at, tile)
            value = own[c, span, :].astype(F32) + rcv0[c, span, :].astype(F32)
            for t in range(steps):
                value += rv[(g, p)][t][k, pl.ds(at, tile), :].astype(F32)
            if last:
                total[span, :] = value
            else:
                own[c, span, :] = value.astype(BF16)

    def send_sum(g, p, k):
        order = SUM_ORDERS[g][p]
        high = k.bit_length() - 1
        step = depth - 1 - high
        gather_terms(g, p, k, step, False)
        copy = pltpu.make_async_remote_copy(
            src_ref=own.at[plan.canon(order, k), pl.ds(g * wide + p * count, count)],
            dst_ref=rv[(g, p)][step].at[k - 2**high],
            send_sem=rs_send.at[0],
            recv_sem=rs_recv.at[g * parts + p, k],
            device_id=others[order[step]],
            device_id_type=MESH,
        )
        copy.start()
        sums[(g, p, k)] = copy

    def update(g):
        for p in range(parts):
            gather_terms(g, p, 0, depth, True)
        once("state", lambda: [load.wait() for load in loads[:3]])
        span = group_span(g)
        gradient = total[span, :].T
        master, first, second = adamw_update(gradient, mw[:, span], m1[:, span], m2[:, span])
        weights[0, g, 0] = master.astype(BF16)
        nm[:, span] = master
        n1[:, span] = first
        n2[:, span] = second
        for i, (s, d) in enumerate([(nm, nm_o), (n1, n1_o), (n2, n2_o)]):
            store = pltpu.make_async_copy(s.at[:, span], d.at[:, span], group_local.at[g, i])
            store.start()
            stores.append(store)

    def pass_on(g, p, q):
        order = GATHER_ORDERS[g][p]
        c = plan.canon(order, q)
        high = q.bit_length() - 1
        if q > 0:
            passed[(g, p, q)].wait_recv()
        rows = pl.ds(p * (R // parts), R // parts)
        for t in range(high + 1, depth):
            e = order[depth - 1 - t]
            copy = pltpu.make_async_remote_copy(
                src_ref=weights.at[0, g, c, rows],
                dst_ref=weights.at[0, g, c + 2**e, rows],
                send_sem=ag_send.at[0],
                recv_sem=ag_recv.at[g * parts + p, q + 2**t],
                device_id=others[e],
                device_id_type=MESH,
            )
            copy.start()
            passed[(g, p, q + 2**t)] = copy
        met[(g, c)] = met.get((g, c), 0) + 1
        if met[(g, c)] == parts:
            copy = pltpu.make_async_remote_copy(
                src_ref=weights.at[0, g, c],
                dst_ref=weights.at[1, g, c],
                send_sem=cg_send.at[0],
                recv_sem=cg_recv.at[g, c],
                device_id=sibling,
                device_id_type=MESH,
            )
            copy.start()
            crossed[(g, c)] = copy

    inner_mask = sum(2**j for j, (axis, _) in enumerate(plan.dims) if axis == "inner")

    def project(side, g, c):
        span = group_span(g)
        if side == 1:
            crossed[(g, c)].wait_recv()
        elif c & inner_mask == 0:
            o, _ = block_at(False, c)
            keep = pltpu.make_async_copy(
                weights.at[0, g, c],
                kept_o.at[pl.ds(pl.multiple_of(o * R, R), R), span],
                group_local.at[g, 3 + c],
            )
            keep.start()
            stores.append(keep)
        once("next", loads[3].wait)
        share = jnp.dot(
            nt[:, columns(side == 1, c)], weights[side, g, c], preferred_element_type=F32
        )
        if ("acc", g) in done:
            acc[:, span] += share
        else:
            done.add(("acc", g))
            acc[:, span] = share

    run = {"T": send_term, "S": send_sum, "F": update, "A": pass_on, "D": project}
    for step in STEPS:
        run[step[0]](*step[1:])
    proj_o[...] = acc[...].astype(BF16)

    sent = [
        (core_send, rcv0),
        (rs_send, own.at[pl.ds(1, blocks - 1)]),
        (ag_send, weights.at[0, :, pl.ds(1, blocks - 1)]),
        (cg_send, weights.at[0]),
    ]
    for sem, ref in sent:
        pltpu.make_async_copy(ref, ref, sem.at[0]).wait()
    for copy in stores:
        copy.wait()


def local_kernel(activations, output_grads, master_weights, first_moment, second_moment, next_tokens):
    n_out, n_in = lax.axis_size("outer"), lax.axis_size("inner")
    tokens, width = activations.shape
    next_rows = next_tokens.shape[0]
    R, C = master_weights.shape
    plan = Plan(n_out, n_in, R, C)
    B, L, G, n_parts = plan.blocks, plan.depth, plan.groups, plan.groups * plan.parts
    dma = pltpu.SemaphoreType.DMA
    any_spec = pl.BlockSpec(memory_space=pl.ANY)
    arrived = [
        pltpu.VMEM((2 ** (L - 1 - s), plan.group_cols // plan.parts, R), BF16)
        for _ in range(n_parts)
        for s in range(L)
    ]
    results = pl.pallas_call(
        functools.partial(kernel, plan),
        out_shape=(
            jax.ShapeDtypeStruct((R, C), F32),
            jax.ShapeDtypeStruct((R, C), F32),
            jax.ShapeDtypeStruct((R, C), F32),
            jax.ShapeDtypeStruct((n_out * R, C), BF16),
            jax.ShapeDtypeStruct((next_rows, C), BF16),
        ),
        in_specs=[any_spec] * 6,
        out_specs=(any_spec,) * 4 + (pl.BlockSpec(memory_space=pltpu.VMEM),),
        scratch_shapes=[
            pltpu.VMEM((2, B, tokens, R), BF16),
            pltpu.VMEM((tokens, C), BF16),
            pltpu.VMEM((next_rows, width), BF16),
        ]
        + [pltpu.VMEM((R, C), F32)] * 6
        + [
            pltpu.VMEM((C, tokens), BF16),
            pltpu.VMEM((B, C, R), BF16),
            pltpu.VMEM((B, C, R), BF16),
            pltpu.VMEM((B, C, R), BF16),
            pltpu.VMEM((C, R), F32),
            pltpu.VMEM((2, G, B, R, plan.group_cols), BF16),
            pltpu.VMEM((next_rows, C), F32),
        ]
        + arrived
        + [
            dma((2, B)),
            dma((1,)),
            dma((G, B)),
            dma((1,)),
            dma((n_parts, B)),
            dma((1,)),
            dma((n_parts, B)),
            dma((1,)),
            dma((G, B)),
            dma((5,)),
            dma((G, 3 + B)),
        ],
        compiler_params=pltpu.CompilerParams(
            collective_id=0, has_side_effects=True, vmem_limit_bytes=58 * 2**20
        ),
        cost_estimate=pl.CostEstimate(
            flops=2 * (tokens + next_rows) * width * C,
            bytes_accessed=2 * (tokens + next_rows) * width + 24 * R * C,
            transcendentals=R * C,
        ),
    )(activations, output_grads, master_weights, first_moment, second_moment, next_tokens)
    return hand_on(results)


def copy_kernel(pieces, *refs):
    count = len(refs) // 3
    sources, targets, held, sems = refs[:count], refs[count : 2 * count], refs[2 * count : -1], refs[-1]
    spans = [
        (i, pl.ds(n * (ref.shape[0] // pieces), ref.shape[0] // pieces))
        for i, ref in enumerate(sources)
        for n in range(pieces)
    ]
    ins = [
        pltpu.make_async_copy(sources[i].at[at], held[i].at[at], sems.at[0, n])
        for n, (i, at) in enumerate(spans)
    ]
    outs = [
        pltpu.make_async_copy(held[i].at[at], targets[i].at[at], sems.at[1, n])
        for n, (i, at) in enumerate(spans)
    ]
    for copy in ins:
        copy.start()
    for copy, onward in zip(ins, outs):
        copy.wait()
        onward.start()
    for copy in outs:
        copy.wait()


def hand_on(arrays, pieces=2):
    any_spec = pl.BlockSpec(memory_space=pl.ANY)
    return pl.pallas_call(
        functools.partial(copy_kernel, pieces),
        out_shape=tuple(jax.ShapeDtypeStruct(a.shape, a.dtype) for a in arrays),
        in_specs=[any_spec] * len(arrays),
        out_specs=(any_spec,) * len(arrays),
        scratch_shapes=[pltpu.VMEM(a.shape, a.dtype) for a in arrays]
        + [pltpu.SemaphoreType.DMA((2, pieces * len(arrays)))],
        compiler_params=pltpu.CompilerParams(vmem_limit_bytes=60 * 2**20),
    )(*arrays)


def fits_kernel(mesh):
    n_out, n_in = mesh.shape["outer"], mesh.shape["inner"]
    return n_out == 8 and n_in == 4


def solution(mesh):
    placed = (
        P(("outer", "inner"), None),
        P(("outer", "inner"), None),
        P(("inner", "outer"), None),
        P(("inner", "outer"), None),
        P(("inner", "outer"), None),
        P(("outer", "inner"), None),
    )
    return jax.shard_map(
        local_kernel if fits_kernel(mesh) else local_plain,
        mesh=mesh,
        in_specs=placed,
        out_specs=(
            P(("inner", "outer"), None),
            P(("inner", "outer"), None),
            P(("inner", "outer"), None),
            P("inner", None),
            P(("outer", "inner"), None),
        ),
        check_vma=False,
    )
```
